32 devices in a mesh: seq: 8 (over z, x), head: 4 (over y, core).
Axes of the slice: x: 2, y: 2, z: 4, core: 2. Of those that a mesh axis runs over, the one named last changes fastest.
Arguments:
- queries: bfloat16 [4096, 16, 128], P('seq', 'head'), may hold values from -6 to 6
- keys: bfloat16 [4096, 16, 128], P('seq', 'head'), may hold values from -6 to 6
- values: bfloat16 [4096, 16, 256], P('seq', 'head'), may hold values from -15 to 15
- beta: float32 [16, 4096], P('head', 'seq'), may hold values from 0 to 0.9
- reset_blocks: int32 [8, 2], P('seq'), may hold values from 0 to 4, as said below
- out_weight: bfloat16 [4096, 4096], P('head'), may hold values from -0.09375 to 0.09375
Outputs:
- layer_out: bfloat16 [4096, 4096], P(('seq', 'head'))
The draws below stay inside these ranges and needn't reach their ends.
Inputs may be any that keep to these rules, and one draw needn't show every extreme that they name: `reset_blocks`: row s lists distinct local indices (0 to 3) of the blocks of sequence shard s at which an episode begins; unused slots hold 4.
All inputs are finite; a program needn't handle non-finite values.
Results may differ from the reference program's by a relative error of at most 0.017.
Values may be sent and summed in bfloat16 or wider, within the bound.
A program may use at most 64 MiB of HBM per device.

```python
import math
import jax
import jax.numpy as jnp
from jax import lax

H = 16
DK = 128
DV = 256
D = 4096
BLOCK = 128
RESETS_MAX = 2
TOK_DEV = 512
TOKENS = 4096
BLOCKS_DEV = 4
SHARDS = 8
N_HEAD = 4


def draw_keys(key, part):
    streams = jax.random.split(key, 3)
    directions = jnp.clip(jax.random.normal(streams[0], (4, H, DK), jnp.float32), -4.0, 4.0)
    weights = jnp.clip(jax.random.normal(streams[1], (TOKENS, H, 4), jnp.float32), -3.0, 3.0)
    drawn = jnp.clip(jax.random.normal(streams[2], (TOKENS, H, DK), jnp.float32) * 0.58, -2.5, 2.5)
    for column in range(4):
        drawn = drawn + 0.5 * weights[:, :, column:column + 1] * directions[column][None, :, :]
    return jnp.clip(drawn, -6.0, 6.0).astype(jnp.bfloat16)


def draw_values(key, part):
    streams = jax.random.split(key, 2)
    scales = jnp.exp(jax.random.uniform(streams[0], (H, DV), jnp.float32) * math.log(10.0)) / 4.0
    noise = jnp.clip(jax.random.normal(streams[1], (TOKENS, H, DV), jnp.float32), -6.0, 6.0)
    drawn = noise * scales[None, :, :]
    return drawn.astype(jnp.bfloat16)


def draw_beta(key, part):
    streams = jax.random.split(key, 5)
    shuffled = jax.random.permutation(streams[0], H)
    position = jnp.argsort(shuffled)
    slow_count = H // 2
    fast_high = 0.3
    rough_low = 0.5
    rough_high = 1.5
    is_slow = position < slow_count
    slow_rate = DK / TOKENS * jnp.exp(jax.random.uniform(streams[1], (H,), jnp.float32, math.log(0.2), math.log(1.5)))
    fast_rate = jnp.exp(jax.random.uniform(streams[2], (H,), jnp.float32, math.log(0.05), math.log(fast_high)))
    head_rate = jnp.where(is_slow, slow_rate, fast_rate)
    shard_rate = jnp.exp(jax.random.uniform(streams[3], (TOKENS // TOK_DEV,), jnp.float32, math.log(0.5), math.log(2.0)))
    token_rate = jnp.repeat(shard_rate, TOK_DEV)
    roughness = jax.random.uniform(streams[4], (H, TOKENS), jnp.float32, rough_low, rough_high)
    return (head_rate[:, None] * token_rate[None, :] * roughness).astype(jnp.float32)


def draw_reset_blocks(key, part):
    streams = jax.random.split(key, 3)
    shard_keys = jax.random.split(streams[0], SHARDS)
    drawn_blocks = jax.vmap(lambda subkey: jax.random.permutation(subkey, BLOCKS_DEV))(shard_keys)[:, :RESETS_MAX]
    leading = (drawn_blocks[0] - drawn_blocks[0, 0]) % BLOCKS_DEV
    drawn_blocks = drawn_blocks.at[0].set(leading)
    target = jax.random.randint(streams[1], (), 1, SHARDS)
    target_fill = jax.random.randint(streams[2], (), 1, RESETS_MAX + 1)
    shard_ids = jnp.arange(SHARDS, dtype=jnp.int32)
    used = jnp.where(shard_ids == target, target_fill, 0).astype(jnp.int32)
    used = used.at[0].set(RESETS_MAX)
    slots = jnp.arange(RESETS_MAX, dtype=jnp.int32)
    filled = jnp.where(slots[None, :] < used[:, None], drawn_blocks, BLOCKS_DEV)
    return filled.astype(jnp.int32)


def block_levels(key, dims, cuts, least, largest):
    def one(dim, parts):
        draws = jax.random.uniform(jax.random.fold_in(jax.random.fold_in(key, 6), dim), (parts,), jnp.float32, least / len(cuts), largest / len(cuts))
        return jnp.repeat(jnp.exp(draws), dims[dim] // parts).reshape((-1,) + (1,) * (len(dims) - dim - 1))

    level = one(*cuts[0])
    for cut in cuts[1:]:
        level = level * one(*cut)
    return level


def normal_values(own_key, shape, scale, reach, shards=(), held_as=jnp.bfloat16):
    values = scale * jax.random.normal(own_key, shape, jnp.float32)
    if shards:
        values = values * block_levels(own_key, shape, shards, -0.22, 0.18)
    return jnp.clip(values, -reach, reach).astype(held_as)


def setup_inputs(seed: int = 0) -> dict:
    seeds = jax.random.split(jax.random.key(seed), 7)
    queries = normal_values(seeds[0], (TOKENS, H, DK), 1.0, 6.0, ((0, 8), (1, 4)))
    keys = draw_keys(jax.random.fold_in(seeds[6], 71), 0)
    values = draw_values(jax.random.fold_in(seeds[6], 71), 0)
    beta = draw_beta(jax.random.fold_in(seeds[6], 71), 0)
    reset_blocks = draw_reset_blocks(jax.random.fold_in(seeds[6], 71), 0)
    out_weight = normal_values(seeds[5], (H * DV, D), (H * DV) ** -0.5, 0.09375, ((0, 4),))
    return {"queries": queries, "keys": keys, "values": values, "beta": beta, "reset_blocks": reset_blocks, "out_weight": out_weight}


exact_precision = lax.Precision.HIGHEST

def unit_rows(values_in, epsilon):
    return values_in * lax.rsqrt(lax.optimization_barrier(jnp.sum(values_in * values_in, axis=-1, keepdims=True)) + epsilon)

def block_terms(query_rows, key_rows, value_rows, rate_rows):
    block_len = key_rows.shape[-2]
    key_dim = key_rows.shape[-1]
    strict = jnp.tril(jnp.ones((block_len, block_len), jnp.float32), -1)
    causal = jnp.tril(jnp.ones((block_len, block_len), jnp.float32))
    key_gram = jnp.einsum('...ik,...jk->...ij', key_rows, key_rows, precision=exact_precision)
    system = jnp.eye(block_len, dtype=jnp.float32) + rate_rows[..., :, None] * key_gram * strict
    right_side = rate_rows[..., :, None] * jnp.concatenate([key_rows, value_rows], axis=-1)
    solved = lax.linalg.triangular_solve(system, right_side, left_side=True, lower=True, unit_diagonal=True)
    attention_scores = jnp.einsum('...ik,...jk->...ij', query_rows, key_rows, precision=exact_precision) * causal
    return (solved[..., :key_dim], solved[..., key_dim:], attention_scores)

def reference(queries, keys, values, beta, reset_blocks, out_weight):
    tokens = queries.shape[0]
    block_count = tokens // BLOCK
    query_rows = unit_rows(queries.astype(jnp.float32), 1e-06).reshape(block_count, BLOCK, H, DK).transpose(0, 2, 1, 3)
    key_rows = unit_rows(keys.astype(jnp.float32), 1e-06).reshape(block_count, BLOCK, H, DK).transpose(0, 2, 1, 3)
    value_rows = values.astype(jnp.float32).reshape(block_count, BLOCK, H, DV).transpose(0, 2, 1, 3)
    rate_rows = beta.reshape(H, block_count, BLOCK).transpose(1, 0, 2)
    local_ids = jnp.arange(BLOCKS_DEV, dtype=jnp.int32)
    starts = jnp.any(reset_blocks[:, :, None] == local_ids[None, None, :], axis=1)
    retain = 1.0 - starts.reshape(block_count).astype(jnp.float32)

    def advance(memory_state, inputs):
        query_block_tile, key_block_tile, v_blk, r_blk, kept = inputs
        decay_rows, update_rows, attention_scores = block_terms(query_block_tile, key_block_tile, v_blk, r_blk)
        memory_state = memory_state * kept
        fresh_value_rows = update_rows - jnp.einsum('gzs,gso->gzo', decay_rows, memory_state, precision=exact_precision)
        output_matrix = jnp.einsum('gzs,gso->gzo', query_block_tile, memory_state, precision=exact_precision) + jnp.einsum('kra,kap->krp', attention_scores, fresh_value_rows, precision=exact_precision)
        memory_state = memory_state + jnp.einsum('glq,glr->gqr', key_block_tile, fresh_value_rows, precision=exact_precision)
        return (memory_state, output_matrix)
    initial = jnp.zeros((H, DK, DV), jnp.float32)
    _, attended = lax.scan(advance, initial, (query_rows, key_rows, value_rows, rate_rows, retain))
    scaled = attended * lax.rsqrt(lax.optimization_barrier(jnp.mean(attended * attended, axis=-1, keepdims=True)) + 1e-05)
    normed = scaled.astype(jnp.bfloat16).transpose(0, 2, 1, 3).reshape(tokens, H * DV)
    group_width = H * DV // N_HEAD
    summed = jnp.zeros((tokens, D), jnp.float32)
    for group_index in range(N_HEAD):
        lo_col = group_index * group_width
        part_sum = jnp.dot(normed[:, lo_col:lo_col + group_width].astype(jnp.float32), out_weight[lo_col:lo_col + group_width].astype(jnp.float32), preferred_element_type=jnp.float32).astype(jnp.bfloat16)
        summed = summed + lax.optimization_barrier(part_sum).astype(jnp.float32)
    return summed.astype(jnp.bfloat16)
```

```python
import functools

import jax
import jax.numpy as jnp
from jax import lax
from jax.experimental import pallas as pl
from jax.experimental.pallas import tpu as pltpu
from jax.sharding import PartitionSpec as P

BLOCK = 128
CHUNK = 512
MESH = pl.DeviceIdType.MESH
F32 = jnp.float32
BF16 = jnp.bfloat16


def dot(a, b):
    return jnp.dot(a, b, preferred_element_type=F32)


def dot_rows(a, b):
    return lax.dot_general(a, b, (((1,), (1,)), ((), ())), preferred_element_type=F32)


def halves(x):
    high = x.astype(BF16)
    return high, (x - high.astype(F32)).astype(BF16)


def exact_left(a, b):
    high, low = halves(b)
    return dot(jnp.concatenate([a, a], axis=1), jnp.concatenate([high, low], axis=0))


def both(a, b):
    ah, al = halves(a)
    bh, bl = halves(b)
    return dot(jnp.concatenate([ah, al, ah], axis=1), jnp.concatenate([bh, bh, bl], axis=0))


def local_kernel(heads, dk, dv, keep_ref, k_ref, q_ref, v_ref, beta_ref, a_ref, d_ref, z_ref):
    b = pl.program_id(0)
    row = lax.broadcasted_iota(jnp.int32, (BLOCK, BLOCK), 0)
    col = lax.broadcasted_iota(jnp.int32, (BLOCK, BLOCK), 1)
    eye = (row == col).astype(F32)

    @pl.when(b == 0)
    def _():
        start = jnp.concatenate([eye, jnp.zeros((dk, dv), F32)], axis=1)
        for h in range(heads):
            z_ref[h] = start

    kept = keep_ref[b]
    ks, rks, lows, scores, rqs, qs = [], [], [], [], [], []
    for h in range(heads):
        k = k_ref[:, h * dk:(h + 1) * dk]
        q = q_ref[:, h * dk:(h + 1) * dk]
        gram = dot_rows(k, k)
        cross = dot_rows(q, k)
        diagonal = gram * eye
        rk = lax.rsqrt(jnp.sum(diagonal, axis=1, keepdims=True) + 1e-6)
        rk_row = lax.rsqrt(jnp.sum(diagonal, axis=0, keepdims=True) + 1e-6)
        q32 = q.astype(F32)
        rq = lax.rsqrt(jnp.sum(q32 * q32, axis=1, keepdims=True) + 1e-6)
        beta = beta_ref[:, h:h + 1]
        lows.append(jnp.where(row > col, gram * (beta * rk) * rk_row, 0.0))
        scores.append(jnp.where(row >= col, cross * rq * rk_row, 0.0))
        ks.append(k)
        qs.append(q)
        rks.append(rk)
        rqs.append(rq)

    inv = [eye - jnp.where((row // 2) == (col // 2), low, 0.0) for low in lows]
    n = 2
    while n < BLOCK:
        cut = ((row // (2 * n)) == (col // (2 * n))) & ((row // n) != (col // n))
        inner = [both(jnp.where(cut, low, 0.0), x) for low, x in zip(lows, inv)]
        inv = [x - both(x, y) for x, y in zip(inv, inner)]
        n *= 2

    zs = [z_ref[h] * kept for h in range(heads)]
    read = [
        exact_left(jnp.concatenate([ks[h], qs[h]], axis=0), zs[h]) for h in range(heads)
    ]
    right = []
    for h in range(heads):
        v = v_ref[:, h * dv:(h + 1) * dv].astype(F32)
        kz = rks[h] * read[h][:BLOCK]
        right.append(
            beta_ref[:, h:h + 1] * jnp.concatenate([-kz[:, :dk], v - kz[:, dk:]], axis=1)
        )
    new = [both(inv[h], right[h]) for h in range(heads)]
    for h in range(heads):
        z_ref[h] = zs[h] + exact_left(ks[h].T, rks[h] * new[h])
    for h in range(heads):
        out = rqs[h] * read[h][BLOCK:] + both(scores[h], new[h])
        a_ref[h] = out[:, :dk].astype(BF16)
        d_ref[h] = out[:, dk:]


def shard_maps(k, q, v, beta, keep, heads, dk, dv):
    tokens = k.shape[0]
    blocks = tokens // BLOCK
    return pl.pallas_call(
        functools.partial(local_kernel, heads, dk, dv),
        grid=(blocks,),
        in_specs=[
            pl.BlockSpec(memory_space=pltpu.SMEM),
            pl.BlockSpec((BLOCK, heads * dk), lambda b: (b, 0)),
            pl.BlockSpec((BLOCK, heads * dk), lambda b: (b, 0)),
            pl.BlockSpec((BLOCK, heads * dv), lambda b: (b, 0)),
            pl.BlockSpec((BLOCK, heads), lambda b: (b, 0)),
        ],
        out_specs=[
            pl.BlockSpec((heads, BLOCK, dk), lambda b: (0, b, 0)),
            pl.BlockSpec((heads, BLOCK, dv), lambda b: (0, b, 0)),
            pl.BlockSpec((heads, dk, dk + dv), lambda b: (0, 0, 0)),
        ],
        out_shape=[
            jax.ShapeDtypeStruct((heads, tokens, dk), BF16),
            jax.ShapeDtypeStruct((heads, tokens, dv), F32),
            jax.ShapeDtypeStruct((heads, dk, dk + dv), F32),
        ],
        compiler_params=pltpu.CompilerParams(vmem_limit_bytes=32 * 1024 * 1024),
        name="shard_maps",
    )(keep, k, q, v, beta)


def relay_kernel(
    shards, groups, heads, dk, dv, chunks,
    a_ref, d_ref, z_ref, w_ref, out_ref,
    w_vmem, came, goes, normed, give1, take1, kept, give2, take2, own,
    w_sem, relay_send, relay_recv, send1, recv1, send2, recv2,
):
    tokens = a_ref.shape[1]
    rows = tokens // groups
    pairs = groups // 2
    half = pairs * rows
    s = lax.axis_index("seq")
    g = lax.axis_index("head")
    y, c = g // 2, g % 2
    mate = y * 2 + (1 - c)

    for j in range(chunks):
        pltpu.make_async_copy(
            w_ref.at[:, pl.ds(j * CHUNK, CHUNK)], w_vmem.at[j], w_sem.at[j]
        ).start()

    barrier = pltpu.get_barrier_semaphore()

    @pl.when(s > 0)
    def _():
        pl.semaphore_signal(barrier, inc=1, device_id={"seq": s - 1}, device_id_type=MESH)

    @pl.when(s < shards - 1)
    def _():
        pl.semaphore_signal(barrier, inc=1, device_id={"seq": s + 1}, device_id_type=MESH)

    pl.semaphore_signal(barrier, inc=1, device_id={"head": mate}, device_id_type=MESH)
    for step in range(1, pairs):
        other = ((y + step) % pairs) * 2 + c
        pl.semaphore_signal(barrier, inc=1, device_id={"head": other}, device_id_type=MESH)

    @pl.when(jnp.logical_and(s > 0, s < shards - 1))
    def _():
        pl.semaphore_wait(barrier, 2 + pairs)

    @pl.when(jnp.logical_or(s == 0, s == shards - 1))
    def _():
        pl.semaphore_wait(barrier, 1 + pairs)

    def relay(h):
        return pltpu.make_async_remote_copy(
            src_ref=goes.at[h], dst_ref=came.at[h],
            send_sem=relay_send.at[h], recv_sem=relay_recv.at[h],
            device_id={"seq": jnp.minimum(s + 1, shards - 1)}, device_id_type=MESH,
        )

    for h in range(heads):
        @pl.when(s == 0)
        def _():
            came[h] = jnp.zeros((dk, dv), BF16)

        @pl.when(s > 0)
        def _():
            relay(h).wait_recv()

        memory = came[h]
        power = z_ref[h, :, :dk]
        high, low = halves(power)
        goes[h] = (
            dot(jnp.concatenate([high, low], axis=1), jnp.concatenate([memory, memory], axis=0))
            + z_ref[h, :, dk:]
        ).astype(BF16)

        @pl.when(s < shards - 1)
        def _():
            relay(h).start()

        attended = dot(a_ref[h], memory) + d_ref[h]
        scale = lax.rsqrt(jnp.mean(attended * attended, axis=1, keepdims=True) + 1e-5)
        result = (attended * scale).astype(BF16)
        for t in range(groups):
            place = jnp.where(c == t % 2, half, 0) + (t // 2) * rows
            normed[pl.ds(pl.multiple_of(place, rows), rows), h * dv:(h + 1) * dv] = result[
                t * rows:(t + 1) * rows
            ]

    def first(j):
        return pltpu.make_async_remote_copy(
            src_ref=give1.at[j], dst_ref=take1.at[j],
            send_sem=send1.at[j], recv_sem=recv1.at[j],
            device_id={"head": mate}, device_id_type=MESH,
        )

    def second(j, step):
        other = (y + step) % pairs
        return pltpu.make_async_remote_copy(
            src_ref=give2.at[j, step - 1], dst_ref=take2.at[j, step - 1],
            send_sem=send2.at[j, step - 1], recv_sem=recv2.at[j, step - 1],
            device_id={"head": other * 2 + c}, device_id_type=MESH,
        )

    def pass_on(j):
        first(j).wait_recv()
        for step in range(1, pairs):
            at = pl.ds(pl.multiple_of(((y + step) % pairs) * rows, rows), rows)
            give2[j, step - 1] = (kept[j, at] + take1[j, at].astype(F32)).astype(BF16)
            second(j, step).start()
        at = pl.ds(pl.multiple_of(y * rows, rows), rows)
        own[j] = kept[j, at] + take1[j, at].astype(F32)

    def project(j, carry):
        pltpu.make_async_copy(
            w_ref.at[:, pl.ds(j * CHUNK, CHUNK)], w_vmem.at[j], w_sem.at[j]
        ).wait()
        part = dot(normed[...], w_vmem[j])
        give1[j] = part[:half].astype(BF16)
        first(j).start()
        kept[j] = part[half:]

        @pl.when(j > 0)
        def _():
            pass_on(j - 1)

        return carry

    lax.fori_loop(0, chunks, project, 0)
    pass_on(chunks - 1)

    for j in range(chunks):
        total = own[j]
        for step in range(1, pairs):
            second(j, step).wait_recv()
            total = total + take2[j, step - 1].astype(F32)
        out_ref[:, j * CHUNK:(j + 1) * CHUNK] = total.astype(BF16)

    for j in range(chunks):
        first(j).wait_send()
        for step in range(1, pairs):
            second(j, step).wait_send()

    @pl.when(s < shards - 1)
    def _():
        for h in range(heads):
            relay(h).wait_send()


def relay_and_project(a, d, z, w, shards, groups, heads, dk, dv):
    tokens = a.shape[1]
    width = w.shape[1]
    chunks = width // CHUNK
    rows = tokens // groups
    pairs = groups // 2
    half = pairs * rows
    far = max(pairs - 1, 1)
    vmem = pl.BlockSpec(memory_space=pltpu.VMEM)
    dma = pltpu.SemaphoreType.DMA
    return pl.pallas_call(
        functools.partial(relay_kernel, shards, groups, heads, dk, dv, chunks),
        in_specs=[vmem, vmem, vmem, pl.BlockSpec(memory_space=pl.ANY)],
        out_specs=vmem,
        out_shape=jax.ShapeDtypeStruct((rows, width), BF16),
        scratch_shapes=[
            pltpu.VMEM((chunks, w.shape[0], CHUNK), BF16),
            pltpu.VMEM((heads, dk, dv), BF16),
            pltpu.VMEM((heads, dk, dv), BF16),
            pltpu.VMEM((tokens, heads * dv), BF16),
            pltpu.VMEM((chunks, half, CHUNK), BF16),
            pltpu.VMEM((chunks, half, CHUNK), BF16),
            pltpu.VMEM((chunks, half, CHUNK), F32),
            pltpu.VMEM((chunks, far, rows, CHUNK), BF16),
            pltpu.VMEM((chunks, far, rows, CHUNK), BF16),
            pltpu.VMEM((chunks, rows, CHUNK), F32),
            dma((chunks,)),
            dma((heads,)),
            dma((heads,)),
            dma((chunks,)),
            dma((chunks,)),
            dma((chunks, far)),
            dma((chunks, far)),
        ],
        compiler_params=pltpu.CompilerParams(
            collective_id=0, has_side_effects=True, vmem_limit_bytes=48 * 1024 * 1024
        ),
        name="relay_and_project",
    )(a, d, z, w)


def body(shards, groups, queries, keys, values, beta, reset_blocks, out_weight):
    tokens, heads, dk = queries.shape
    dv = values.shape[2]
    blocks = tokens // BLOCK
    starts = jnp.any(
        reset_blocks[0][:, None] == jnp.arange(blocks, dtype=jnp.int32)[None, :], axis=0
    )
    keep = 1.0 - starts.astype(F32)
    a, d, z = shard_maps(
        keys.reshape(tokens, heads * dk),
        queries.reshape(tokens, heads * dk),
        values.reshape(tokens, heads * dv),
        beta.T,
        keep,
        heads, dk, dv,
    )
    return relay_and_project(a, d, z, out_weight, shards, groups, heads, dk, dv)


def solution(mesh):
    return jax.shard_map(
        functools.partial(body, mesh.shape["seq"], mesh.shape["head"]),
        mesh=mesh,
        in_specs=(
            P("seq", "head", None),
            P("seq", "head", None),
            P("seq", "head", None),
            P("head", "seq"),
            P("seq", None),
            P("head", None),
        ),
        out_specs=P(("seq", "head"), None),
        check_vma=False,
    )
```

```python
import functools

import jax
import jax.numpy as jnp
from jax import lax
from jax.experimental import pallas as pl
from jax.experimental.pallas import tpu as pltpu
from jax.sharding import PartitionSpec as P

BLOCK = 128
CHUNK = 512
MESH = pl.DeviceIdType.MESH
F32 = jnp.float32
BF16 = jnp.bfloat16


def dot(a, b):
    return jnp.dot(a, b, preferred_element_type=F32)


def dot_rows(a, b):
    return lax.dot_general(a, b, (((1,), (1,)), ((), ())), preferred_element_type=F32)


def rounded(a, b):
    return dot(a.astype(BF16), b.astype(BF16))


def local_kernel(
    heads, dk, dv, reset_ref, k_ref, q_ref, v_ref, beta_ref, a_ref, d_ref, z_ref, send_ref
):
    b = pl.program_id(0)
    row = lax.broadcasted_iota(jnp.int32, (BLOCK, BLOCK), 0)
    col = lax.broadcasted_iota(jnp.int32, (BLOCK, BLOCK), 1)
    eye = (row == col).astype(F32)

    @pl.when(b == 0)
    def _():
        start = jnp.concatenate([eye, jnp.zeros((dk, dv), F32)], axis=1)
        for h in range(heads):
            z_ref[h] = start

    kept = jnp.float32(1.0)
    for slot in range(reset_ref.shape[1]):
        kept = jnp.where(reset_ref[0, slot] == b, 0.0, kept)
    ks, rks, lows, scores, rqs, qs = [], [], [], [], [], []
    for h in range(heads):
        k = k_ref[:, h * dk:(h + 1) * dk]
        q = q_ref[:, h * dk:(h + 1) * dk]
        gram = dot_rows(k, k)
        cross = dot_rows(q, k)
        diagonal = gram * eye
        rk = lax.rsqrt(jnp.sum(diagonal, axis=1, keepdims=True) + 1e-6)
        rk_row = lax.rsqrt(jnp.sum(diagonal, axis=0, keepdims=True) + 1e-6)
        q32 = q.astype(F32)
        rq = lax.rsqrt(jnp.sum(q32 * q32, axis=1, keepdims=True) + 1e-6)
        beta = beta_ref[:, h:h + 1]
        lows.append(jnp.where(row > col, gram * (beta * rk) * rk_row, 0.0))
        scores.append(jnp.where(row >= col, cross * rq * rk_row, 0.0))
        ks.append(k)
        qs.append(q)
        rks.append(rk)
        rqs.append(rq)

    inv = [eye - jnp.where((row // 2) == (col // 2), low, 0.0) for low in lows]
    n = 2
    while n < BLOCK:
        cut = ((row // (2 * n)) == (col // (2 * n))) & ((row // n) != (col // n))
        inner = [rounded(jnp.where(cut, low, 0.0), x) for low, x in zip(lows, inv)]
        inv = [x - rounded(x, y) for x, y in zip(inv, inner)]
        n *= 2

    zs = [z_ref[h] * kept for h in range(heads)]
    read = [
        rounded(jnp.concatenate([ks[h], qs[h]], axis=0), zs[h]) for h in range(heads)
    ]
    right = []
    for h in range(heads):
        v = v_ref[:, h * dv:(h + 1) * dv].astype(F32)
        kz = rks[h] * read[h][:BLOCK]
        right.append(
            beta_ref[:, h:h + 1] * jnp.concatenate([-kz[:, :dk], v - kz[:, dk:]], axis=1)
        )
    new = [rounded(inv[h], right[h]) for h in range(heads)]
    for h in range(heads):
        z_ref[h] = zs[h] + rounded(ks[h].T, rks[h] * new[h])
        send_ref[h] = z_ref[h].astype(BF16)
    for h in range(heads):
        out = rqs[h] * read[h][BLOCK:] + rounded(scores[h], new[h])
        a_ref[h] = out[:, :dk].astype(BF16)
        d_ref[h] = out[:, dk:]


def shard_maps(k, q, v, beta, resets, heads, dk, dv):
    tokens = k.shape[0]
    blocks = tokens // BLOCK
    return pl.pallas_call(
        functools.partial(local_kernel, heads, dk, dv),
        grid=(blocks,),
        in_specs=[
            pl.BlockSpec(memory_space=pltpu.SMEM),
            pl.BlockSpec((BLOCK, heads * dk), lambda b: (b, 0)),
            pl.BlockSpec((BLOCK, heads * dk), lambda b: (b, 0)),
            pl.BlockSpec((BLOCK, heads * dv), lambda b: (b, 0)),
            pl.BlockSpec((BLOCK, heads), lambda b: (b, 0)),
        ],
        out_specs=[
            pl.BlockSpec((heads, BLOCK, dk), lambda b: (0, b, 0)),
            pl.BlockSpec((heads, BLOCK, dv), lambda b: (0, b, 0)),
            pl.BlockSpec((heads, dk, dk + dv), lambda b: (0, 0, 0)),
            pl.BlockSpec((heads, dk, dk + dv), lambda b: (0, 0, 0)),
        ],
        out_shape=[
            jax.ShapeDtypeStruct((heads, tokens, dk), BF16),
            jax.ShapeDtypeStruct((heads, tokens, dv), F32),
            jax.ShapeDtypeStruct((heads, dk, dk + dv), F32),
            jax.ShapeDtypeStruct((heads, dk, dk + dv), BF16),
        ],
        compiler_params=pltpu.CompilerParams(vmem_limit_bytes=32 * 1024 * 1024),
        name="shard_maps",
    )(resets, k, q, v, beta)


def relay_kernel(
    shards, groups, heads, dk, dv, chunks,
    a_ref, d_ref, z_ref, zb_ref, w_ref, out_ref,
    w_vmem, before, joined, chain, came, goes, normed, give1, take1, kept, give2, take2, own,
    w_sem, pair_send, pair_recv, chain_send, chain_recv, step_send, step_recv, send1, recv1, send2, recv2,
):
    tokens = a_ref.shape[1]
    rows = tokens // groups
    pairs = groups // 2
    half = pairs * rows
    s = lax.axis_index("seq")
    g = lax.axis_index("head")
    y, c = g // 2, g % 2
    mate = y * 2 + (1 - c)

    for j in range(chunks):
        pltpu.make_async_copy(
            w_ref.at[:, pl.ds(j * CHUNK, CHUNK)], w_vmem.at[j], w_sem.at[j]
        ).start()

    odd = s % 2 == 1
    even = s % 2 == 0
    ahead = s < shards - 2

    barrier = pltpu.get_barrier_semaphore()

    def greet(**place):
        pl.semaphore_signal(barrier, inc=1, device_id=place, device_id_type=MESH)

    @pl.when(even)
    def _():
        greet(seq=s + 1)

    @pl.when(jnp.logical_and(even, s > 0))
    def _():
        greet(seq=s - 1)

    @pl.when(odd)
    def _():
        greet(seq=s - 1)

    @pl.when(jnp.logical_and(odd, ahead))
    def _():
        greet(seq=s + 1)
        greet(seq=s + 2)

    @pl.when(jnp.logical_and(odd, s > 1))
    def _():
        greet(seq=s - 2)

    greet(head=mate)
    for step in range(1, pairs):
        greet(head=((y + step) % pairs) * 2 + c)

    @pl.when(even)
    def _():
        pl.semaphore_wait(barrier, pairs + 1 + jnp.where(s > 0, 1, 0))

    @pl.when(odd)
    def _():
        pl.semaphore_wait(
            barrier, pairs + 1 + jnp.where(ahead, 2, 0) + jnp.where(s > 1, 1, 0)
        )

    def to_pair(h):
        return pltpu.make_async_remote_copy(
            src_ref=zb_ref.at[h], dst_ref=before.at[h],
            send_sem=pair_send.at[h], recv_sem=pair_recv.at[h],
            device_id={"seq": jnp.minimum(s + 1, shards - 1)}, device_id_type=MESH,
        )

    def to_chain(h):
        return pltpu.make_async_remote_copy(
            src_ref=goes.at[h], dst_ref=chain.at[h],
            send_sem=chain_send.at[h], recv_sem=chain_recv.at[h],
            device_id={"seq": jnp.minimum(s + 2, shards - 1)}, device_id_type=MESH,
        )

    def to_next(h):
        return pltpu.make_async_remote_copy(
            src_ref=goes.at[h], dst_ref=came.at[h],
            send_sem=step_send.at[h], recv_sem=step_recv.at[h],
            device_id={"seq": jnp.minimum(s + 1, shards - 1)}, device_id_type=MESH,
        )

    def hand_on(h):
        @pl.when(ahead)
        def _():
            to_chain(h).start()
            to_next(h).start()

    @pl.when(even)
    def _():
        for h in range(heads):
            to_pair(h).start()

    def join(h):
        @pl.when(odd)
        def _():
            to_pair(h).wait_recv()
            both = dot(zb_ref[h, :, :dk], before[h])
            joined[h, :, :dk] = both[:, :dk]
            joined[h, :, dk:] = both[:, dk:] + z_ref[h, :, dk:]

        @pl.when(s == 1)
        def _():
            goes[h] = joined[h, :, dk:].astype(BF16)
            hand_on(h)
            came[h] = before[h, :, dk:]

    join(0)
    for h in range(heads):
        if h + 1 < heads:
            join(h + 1)

        @pl.when(jnp.logical_and(odd, s > 1))
        def _():
            to_chain(h).wait_recv()
            goes[h] = (
                dot(joined[h, :, :dk].astype(BF16), chain[h]) + joined[h, :, dk:]
            ).astype(BF16)
            hand_on(h)
            came[h] = (
                dot(before[h, :, :dk], chain[h]) + before[h, :, dk:].astype(F32)
            ).astype(BF16)

        @pl.when(s == 0)
        def _():
            came[h] = jnp.zeros((dk, dv), BF16)

        @pl.when(jnp.logical_and(even, s > 0))
        def _():
            to_next(h).wait_recv()

        attended = dot(a_ref[h], came[h]) + d_ref[h]
        scale = lax.rsqrt(jnp.mean(attended * attended, axis=1, keepdims=True) + 1e-5)
        result = (attended * scale).astype(BF16)
        for t in range(groups):
            place = jnp.where(c == t % 2, half, 0) + (t // 2) * rows
            normed[pl.ds(pl.multiple_of(place, rows), rows), h * dv:(h + 1) * dv] = result[
                t * rows:(t + 1) * rows
            ]

    def first(j):
        return pltpu.make_async_remote_copy(
            src_ref=give1.at[j], dst_ref=take1.at[j],
            send_sem=send1.at[j], recv_sem=recv1.at[j],
            device_id={"head": mate}, device_id_type=MESH,
        )

    def second(j, step):
        other = (y + step) % pairs
        return pltpu.make_async_remote_copy(
            src_ref=give2.at[j, step - 1], dst_ref=take2.at[j, step - 1],
            send_sem=send2.at[j, step - 1], recv_sem=recv2.at[j, step - 1],
            device_id={"head": other * 2 + c}, device_id_type=MESH,
        )

    def pass_on(j):
        first(j).wait_recv()
        for step in range(1, pairs):
            at = pl.ds(pl.multiple_of(((y + step) % pairs) * rows, rows), rows)
            give2[j, step - 1] = (kept[j, at] + take1[j, at].astype(F32)).astype(BF16)
            second(j, step).start()
        at = pl.ds(pl.multiple_of(y * rows, rows), rows)
        own[j] = kept[j, at] + take1[j, at].astype(F32)

    def project(j, carry):
        pltpu.make_async_copy(
            w_ref.at[:, pl.ds(j * CHUNK, CHUNK)], w_vmem.at[j], w_sem.at[j]
        ).wait()
        part = dot(normed[...], w_vmem[j])
        give1[j] = part[:half].astype(BF16)
        first(j).start()
        kept[j] = part[half:]

        @pl.when(j > 0)
        def _():
            pass_on(j - 1)

        return carry

    lax.fori_loop(0, chunks, project, 0)
    pass_on(chunks - 1)

    for j in range(chunks):
        total = own[j]
        for step in range(1, pairs):
            second(j, step).wait_recv()
            total = total + take2[j, step - 1].astype(F32)
        out_ref[:, j * CHUNK:(j + 1) * CHUNK] = total.astype(BF16)

    for j in range(chunks):
        first(j).wait_send()
        for step in range(1, pairs):
            second(j, step).wait_send()

    @pl.when(even)
    def _():
        for h in range(heads):
            to_pair(h).wait_send()

    @pl.when(jnp.logical_and(odd, ahead))
    def _():
        for h in range(heads):
            to_chain(h).wait_send()
            to_next(h).wait_send()


def relay_and_project(a, d, z, zb, w, shards, groups, heads, dk, dv):
    tokens = a.shape[1]
    width = w.shape[1]
    chunks = width // CHUNK
    rows = tokens // groups
    pairs = groups // 2
    half = pairs * rows
    far = max(pairs - 1, 1)
    vmem = pl.BlockSpec(memory_space=pltpu.VMEM)
    dma = pltpu.SemaphoreType.DMA
    return pl.pallas_call(
        functools.partial(relay_kernel, shards, groups, heads, dk, dv, chunks),
        in_specs=[vmem, vmem, vmem, vmem, pl.BlockSpec(memory_space=pl.ANY)],
        out_specs=vmem,
        out_shape=jax.ShapeDtypeStruct((rows, width), BF16),
        scratch_shapes=[
            pltpu.VMEM((chunks, w.shape[0], CHUNK), BF16),
            pltpu.VMEM((heads, dk, dk + dv), BF16),
            pltpu.VMEM((heads, dk, dk + dv), F32),
            pltpu.VMEM((heads, dk, dv), BF16),
            pltpu.VMEM((heads, dk, dv), BF16),
            pltpu.VMEM((heads, dk, dv), BF16),
            pltpu.VMEM((tokens, heads * dv), BF16),
            pltpu.VMEM((chunks, half, CHUNK), BF16),
            pltpu.VMEM((chunks, half, CHUNK), BF16),
            pltpu.VMEM((chunks, half, CHUNK), F32),
            pltpu.VMEM((chunks, far, rows, CHUNK), BF16),
            pltpu.VMEM((chunks, far, rows, CHUNK), BF16),
            pltpu.VMEM((chunks, rows, CHUNK), F32),
            dma((chunks,)),
            dma((heads,)),
            dma((heads,)),
            dma((heads,)),
            dma((heads,)),
            dma((heads,)),
            dma((heads,)),
            dma((chunks,)),
            dma((chunks,)),
            dma((chunks, far)),
            dma((chunks, far)),
        ],
        compiler_params=pltpu.CompilerParams(
            collective_id=0, has_side_effects=True, vmem_limit_bytes=48 * 1024 * 1024
        ),
        name="relay_and_project",
    )(a, d, z, zb, w)


def body(shards, groups, queries, keys, values, beta, reset_blocks, out_weight):
    tokens, heads, dk = queries.shape
    dv = values.shape[2]
    a, d, z, zb = shard_maps(
        keys.reshape(tokens, heads * dk),
        queries.reshape(tokens, heads * dk),
        values.reshape(tokens, heads * dv),
        beta.T,
        reset_blocks,
        heads, dk, dv,
    )
    return relay_and_project(a, d, z, zb, out_weight, shards, groups, heads, dk, dv)


def solution(mesh):
    return jax.shard_map(
        functools.partial(body, mesh.shape["seq"], mesh.shape["head"]),
        mesh=mesh,
        in_specs=(
            P("seq", "head", None),
            P("seq", "head", None),
            P("seq", "head", None),
            P("head", "seq"),
            P("seq", None),
            P("head", None),
        ),
        out_specs=P(("seq", "head"), None),
        check_vma=False,
    )
```

```python
import functools

import jax
import jax.numpy as jnp
from jax import lax
from jax.experimental import pallas as pl
from jax.experimental.pallas import tpu as pltpu
from jax.sharding import PartitionSpec as P

BLOCK = 128
CHUNK = 512
MESH = pl.DeviceIdType.MESH
F32 = jnp.float32
BF16 = jnp.bfloat16


def dot(a, b):
    return jnp.dot(a, b, preferred_element_type=F32)


def dot_rows(a, b):
    return lax.dot_general(a, b, (((1,), (1,)), ((), ())), preferred_element_type=F32)


def rounded(a, b):
    return dot(a.astype(BF16), b.astype(BF16))


def local_kernel(
    lanes, blocks, dk, dv, reset_ref, k_ref, q_ref, v_ref, beta_ref, a_ref, d_ref, z_ref, send_ref
):
    base = pl.program_id(0) * lanes
    row = lax.broadcasted_iota(jnp.int32, (BLOCK, BLOCK), 0)
    col = lax.broadcasted_iota(jnp.int32, (BLOCK, BLOCK), 1)
    diagonal = row == col
    eye = diagonal.astype(F32)
    items = [(h, b) for b in range(blocks) for h in range(lanes)]

    ks, qs, rks, rk_rows, rqs, betas, lows, scores = [], [], [], [], [], [], [], []
    for h, b in items:
        at = slice(b * BLOCK, (b + 1) * BLOCK)
        k = k_ref[at, h * dk:(h + 1) * dk]
        q = q_ref[at, h * dk:(h + 1) * dk]
        products = dot_rows(jnp.concatenate([k, q], axis=0), k)
        gram, cross = products[:BLOCK], products[BLOCK:]
        squares = jnp.where(diagonal, gram, 0.0)
        rk = lax.rsqrt(jnp.sum(squares, axis=1, keepdims=True) + 1e-6)
        rk_row = lax.rsqrt(jnp.sum(squares, axis=0, keepdims=True) + 1e-6)
        q32 = q.astype(F32)
        rq = lax.rsqrt(jnp.sum(q32 * q32, axis=1, keepdims=True) + 1e-6)
        every = beta_ref[:, at]
        wanted = lax.broadcasted_iota(jnp.int32, every.shape, 0) == base + h
        beta_row = jnp.sum(jnp.where(wanted, every, 0.0), axis=0, keepdims=True)
        beta = jnp.sum(jnp.where(diagonal, beta_row, 0.0), axis=1, keepdims=True)
        lows.append(jnp.where(row > col, gram * (beta * rk) * rk_row, 0.0))
        scores.append(jnp.where(row >= col, cross * rq, 0.0).astype(BF16))
        ks.append(k)
        qs.append(q)
        rks.append(rk)
        rk_rows.append(rk_row)
        rqs.append(rq)
        betas.append(beta_row)

    inv = []
    for low in lows:
        pairs = jnp.where((row // 2) == (col // 2), low, 0.0)
        cut = jnp.where(((row // 4) == (col // 4)) & ((row // 2) != (col // 2)), low, 0.0)
        inner = cut - pltpu.roll(cut, BLOCK - 1, 1) * jnp.sum(pairs, axis=0, keepdims=True)
        inner = inner - pltpu.roll(inner, 1, 0) * jnp.sum(pairs, axis=1, keepdims=True)
        inv.append(eye - pairs - inner)
    n = 4
    while n < BLOCK:
        cut = ((row // (2 * n)) == (col // (2 * n))) & ((row // n) != (col // n))
        narrow = [x.astype(BF16) for x in inv]
        inner = [
            dot(jnp.where(cut, low, 0.0).astype(BF16), x).astype(BF16)
            for low, x in zip(lows, narrow)
        ]
        inv = [x - dot(y, z) for x, y, z in zip(inv, narrow, inner)]
        n *= 2

    solved = []
    for (h, b), k, x, rk, rk_row, beta in zip(items, ks, inv, rks, rk_rows, betas):
        v = v_ref[b * BLOCK:(b + 1) * BLOCK, h * dv:(h + 1) * dv]
        scaled = x * beta
        solved.append(
            jnp.concatenate(
                [rk * rounded(scaled * rk_row, k), rk * rounded(scaled, v)], axis=1
            ).astype(BF16)
        )
    parts = [
        dot(jnp.concatenate([k.T, score], axis=0), wu)
        for k, score, wu in zip(ks, scores, solved)
    ]

    zs = [None] * lanes
    for (h, b), q, rq, part in zip(items, qs, rqs, parts):
        kept = jnp.float32(1.0)
        for slot in range(reset_ref.shape[1]):
            kept = jnp.where(reset_ref[0, slot] == b, 0.0, kept)
        take = part[:dk, :dk]
        read = rq * q.astype(F32) - part[dk:, :dk]
        if b == 0:
            linear = kept * (eye - take)
            constant = part[:dk, dk:]
            out_linear = kept * read
            out_constant = part[dk:, dk:]
        else:
            z = zs[h] * kept
            moved = rounded(jnp.concatenate([take, read], axis=0), z)
            linear = z[:, :dk] - moved[:dk, :dk]
            constant = z[:, dk:] - moved[:dk, dk:] + part[:dk, dk:]
            out_linear = moved[dk:, :dk]
            out_constant = moved[dk:, dk:] + part[dk:, dk:]
        zs[h] = jnp.concatenate([linear, constant], axis=1)
        a_ref[h, b * BLOCK:(b + 1) * BLOCK] = out_linear.astype(BF16)
        d_ref[h, b * BLOCK:(b + 1) * BLOCK] = out_constant.astype(BF16)
    for h in range(lanes):
        z_ref[h] = zs[h][:, dk:]
        send_ref[h] = zs[h].astype(BF16)


def shard_maps(k, q, v, beta, resets, heads, dk, dv):
    tokens = k.shape[0]
    lanes = 2
    return pl.pallas_call(
        functools.partial(local_kernel, lanes, tokens // BLOCK, dk, dv),
        grid=(heads // lanes,),
        in_specs=[
            pl.BlockSpec(memory_space=pltpu.SMEM),
            pl.BlockSpec((tokens, lanes * dk), lambda i: (0, i)),
            pl.BlockSpec((tokens, lanes * dk), lambda i: (0, i)),
            pl.BlockSpec((tokens, lanes * dv), lambda i: (0, i)),
            pl.BlockSpec((heads, tokens), lambda i: (0, 0)),
        ],
        out_specs=[
            pl.BlockSpec((lanes, tokens, dk), lambda i: (i, 0, 0)),
            pl.BlockSpec((lanes, tokens, dv), lambda i: (i, 0, 0)),
            pl.BlockSpec((lanes, dk, dv), lambda i: (i, 0, 0)),
            pl.BlockSpec((lanes, dk, dk + dv), lambda i: (i, 0, 0)),
        ],
        out_shape=[
            jax.ShapeDtypeStruct((heads, tokens, dk), BF16),
            jax.ShapeDtypeStruct((heads, tokens, dv), BF16),
            jax.ShapeDtypeStruct((heads, dk, dv), F32),
            jax.ShapeDtypeStruct((heads, dk, dk + dv), BF16),
        ],
        compiler_params=pltpu.CompilerParams(vmem_limit_bytes=40 * 1024 * 1024),
        name="shard_maps",
    )(resets, k, q, v, beta)


def relay_kernel(
    shards, groups, heads, dk, dv, chunks,
    a_ref, d_ref, z_ref, zb_ref, w_ref, out_ref,
    w_vmem, before, joined, chain, came, goes, hands, normed, give1, take1, kept, give2, take2, own,
    w_sem, pair_send, pair_recv, chain_send, chain_recv, step_send, step_recv, send1, recv1, send2, recv2,
):
    tokens = a_ref.shape[1]
    rows = tokens // groups
    pairs = groups // 2
    half = pairs * rows
    s = lax.axis_index("seq")
    g = lax.axis_index("head")
    y, c = g // 2, g % 2
    mate = y * 2 + (1 - c)

    for j in range(chunks):
        pltpu.make_async_copy(
            w_ref.at[:, pl.ds(j * CHUNK, CHUNK)], w_vmem.at[j], w_sem.at[j]
        ).start()

    share = heads // 2
    parity = s % 2
    odd = parity == 1
    partner = s + 1 - 2 * parity

    def mine(i):
        return (1 - parity) * share + i

    def theirs(i):
        return parity * share + i

    barrier = pltpu.get_barrier_semaphore()

    def greet(**place):
        pl.semaphore_signal(barrier, inc=1, device_id=place, device_id_type=MESH)

    for gap in (1, 2):
        @pl.when(s >= gap)
        def _():
            greet(seq=s - gap)

        @pl.when(s < shards - gap)
        def _():
            greet(seq=s + gap)

    greet(head=mate)
    for step in range(1, pairs):
        greet(head=((y + step) % pairs) * 2 + c)
    pl.semaphore_wait(
        barrier,
        pairs
        + jnp.where(s >= 1, 1, 0) + jnp.where(s >= 2, 1, 0)
        + jnp.where(s < shards - 1, 1, 0) + jnp.where(s < shards - 2, 1, 0),
    )

    def to_partner(i):
        return pltpu.make_async_remote_copy(
            src_ref=zb_ref.at[theirs(i)], dst_ref=before.at[i],
            send_sem=pair_send.at[i], recv_sem=pair_recv.at[i],
            device_id={"seq": partner}, device_id_type=MESH,
        )

    def to_chain(i):
        return pltpu.make_async_remote_copy(
            src_ref=goes.at[i], dst_ref=chain.at[i],
            send_sem=chain_send.at[i], recv_sem=chain_recv.at[i],
            device_id={"seq": jnp.minimum(s + 2, shards - 1)}, device_id_type=MESH,
        )

    def to_next(i):
        return pltpu.make_async_remote_copy(
            src_ref=hands.at[i], dst_ref=came.at[i],
            send_sem=step_send.at[i], recv_sem=step_recv.at[i],
            device_id={"seq": jnp.minimum(s + 1, shards - 1)}, device_id_type=MESH,
        )

    for i in range(share):
        to_partner(i).start()

    def replay(h, memory):
        attended = dot(a_ref[h], memory) + d_ref[h].astype(F32)
        scale = lax.rsqrt(jnp.mean(attended * attended, axis=1, keepdims=True) + 1e-5)
        result = (attended * scale).astype(BF16)
        columns = pl.ds(pl.multiple_of(h * dv, dv), dv)
        for t in range(groups):
            place = jnp.where(c == t % 2, half, 0) + (t // 2) * rows
            normed[pl.ds(pl.multiple_of(place, rows), rows), columns] = result[
                t * rows:(t + 1) * rows
            ]

    for i in range(share):
        h = mine(i)
        to_partner(i).wait_recv()

        @pl.when(odd)
        def _():
            both = dot(zb_ref[h, :, :dk], before[i])
            joined[i, :, :dk] = both[:, :dk]
            joined[i, :, dk:] = both[:, dk:] + z_ref[h]

        @pl.when(jnp.logical_not(odd))
        def _():
            both = dot(before[i, :, :dk], zb_ref[h])
            joined[i, :, :dk] = both[:, :dk]
            joined[i, :, dk:] = both[:, dk:] + before[i, :, dk:].astype(F32)

        @pl.when(s < 2)
        def _():
            chain[i] = jnp.zeros((dk, dv), BF16)

        @pl.when(s >= 2)
        def _():
            to_chain(i).wait_recv()

        goes[i] = (
            dot(joined[i, :, :dk].astype(BF16), chain[i]) + joined[i, :, dk:]
        ).astype(BF16)

        @pl.when(s < shards - 2)
        def _():
            to_chain(i).start()

        @pl.when(odd)
        def _():
            hands[i] = goes[i]
            joined[i, :, dk:] = (
                dot(before[i, :, :dk], chain[i]) + before[i, :, dk:].astype(F32)
            )

        @pl.when(jnp.logical_not(odd))
        def _():
            hands[i] = (dot(zb_ref[h, :, :dk], chain[i]) + z_ref[h]).astype(BF16)
            joined[i, :, dk:] = chain[i].astype(F32)

        @pl.when(s < shards - 1)
        def _():
            to_next(i).start()

    for i in range(share):
        replay(mine(i), joined[i, :, dk:].astype(BF16))

    for i in range(share):
        @pl.when(s == 0)
        def _():
            came[i] = jnp.zeros((dk, dv), BF16)

        @pl.when(s > 0)
        def _():
            to_next(i).wait_recv()

        replay(theirs(i), came[i])

    def first(j):
        return pltpu.make_async_remote_copy(
            src_ref=give1.at[j], dst_ref=take1.at[j],
            send_sem=send1.at[j], recv_sem=recv1.at[j],
            device_id={"head": mate}, device_id_type=MESH,
        )

    def second(j, step):
        other = (y + step) % pairs
        return pltpu.make_async_remote_copy(
            src_ref=give2.at[j, step - 1], dst_ref=take2.at[j, step - 1],
            send_sem=send2.at[j, step - 1], recv_sem=recv2.at[j, step - 1],
            device_id={"head": other * 2 + c}, device_id_type=MESH,
        )

    def pass_on(j):
        first(j).wait_recv()
        for step in range(1, pairs):
            at = pl.ds(pl.multiple_of(((y + step) % pairs) * rows, rows), rows)
            give2[j, step - 1] = (kept[j, at] + take1[j, at].astype(F32)).astype(BF16)
            second(j, step).start()
        at = pl.ds(pl.multiple_of(y * rows, rows), rows)
        own[j] = kept[j, at] + take1[j, at].astype(F32)

    def project(j, carry):
        pltpu.make_async_copy(
            w_ref.at[:, pl.ds(j * CHUNK, CHUNK)], w_vmem.at[j], w_sem.at[j]
        ).wait()
        part = dot(normed[...], w_vmem[j])
        give1[j] = part[:half].astype(BF16)
        first(j).start()
        kept[j] = part[half:]

        @pl.when(j > 0)
        def _():
            pass_on(j - 1)

        return carry

    lax.fori_loop(0, chunks, project, 0)
    pass_on(chunks - 1)

    for j in range(chunks):
        total = own[j]
        for step in range(1, pairs):
            second(j, step).wait_recv()
            total = total + take2[j, step - 1].astype(F32)
        out_ref[:, j * CHUNK:(j + 1) * CHUNK] = total.astype(BF16)

    for j in range(chunks):
        first(j).wait_send()
        for step in range(1, pairs):
            second(j, step).wait_send()

    for i in range(share):
        to_partner(i).wait_send()

    @pl.when(s < shards - 2)
    def _():
        for i in range(share):
            to_chain(i).wait_send()

    @pl.when(s < shards - 1)
    def _():
        for i in range(share):
            to_next(i).wait_send()


def relay_and_project(a, d, z, zb, w, shards, groups, heads, dk, dv):
    tokens = a.shape[1]
    width = w.shape[1]
    chunks = width // CHUNK
    rows = tokens // groups
    pairs = groups // 2
    half = pairs * rows
    far = max(pairs - 1, 1)
    share = heads // 2
    vmem = pl.BlockSpec(memory_space=pltpu.VMEM)
    dma = pltpu.SemaphoreType.DMA
    return pl.pallas_call(
        functools.partial(relay_kernel, shards, groups, heads, dk, dv, chunks),
        in_specs=[vmem, vmem, vmem, vmem, pl.BlockSpec(memory_space=pl.ANY)],
        out_specs=vmem,
        out_shape=jax.ShapeDtypeStruct((rows, width), BF16),
        scratch_shapes=[
            pltpu.VMEM((chunks, w.shape[0], CHUNK), BF16),
            pltpu.VMEM((share, dk, dk + dv), BF16),
            pltpu.VMEM((share, dk, dk + dv), F32),
            pltpu.VMEM((share, dk, dv), BF16),
            pltpu.VMEM((share, dk, dv), BF16),
            pltpu.VMEM((share, dk, dv), BF16),
            pltpu.VMEM((share, dk, dv), BF16),
            pltpu.VMEM((tokens, heads * dv), BF16),
            pltpu.VMEM((chunks, half, CHUNK), BF16),
            pltpu.VMEM((chunks, half, CHUNK), BF16),
            pltpu.VMEM((chunks, half, CHUNK), F32),
            pltpu.VMEM((chunks, far, rows, CHUNK), BF16),
            pltpu.VMEM((chunks, far, rows, CHUNK), BF16),
            pltpu.VMEM((chunks, rows, CHUNK), F32),
            dma((chunks,)),
            dma((share,)),
            dma((share,)),
            dma((share,)),
            dma((share,)),
            dma((share,)),
            dma((share,)),
            dma((chunks,)),
            dma((chunks,)),
            dma((chunks, far)),
            dma((chunks, far)),
        ],
        compiler_params=pltpu.CompilerParams(
            collective_id=0, has_side_effects=True, vmem_limit_bytes=48 * 1024 * 1024
        ),
        name="relay_and_project",
    )(a, d, z, zb, w)


def body(shards, groups, queries, keys, values, beta, reset_blocks, out_weight):
    tokens, heads, dk = queries.shape
    dv = values.shape[2]
    a, d, z, zb = shard_maps(
        keys.reshape(tokens, heads * dk),
        queries.reshape(tokens, heads * dk),
        values.reshape(tokens, heads * dv),
        beta,
        reset_blocks,
        heads, dk, dv,
    )
    return relay_and_project(a, d, z, zb, out_weight, shards, groups, heads, dk, dv)


def solution(mesh):
    return jax.shard_map(
        functools.partial(body, mesh.shape["seq"], mesh.shape["head"]),
        mesh=mesh,
        in_specs=(
            P("seq", "head", None),
            P("seq", "head", None),
            P("seq", "head", None),
            P("head", "seq"),
            P("seq", None),
            P("head", None),
        ),
        out_specs=P(("seq", "head"), None),
        check_vma=False,
    )
```

```python
import functools

import jax
import jax.numpy as jnp
from jax import lax
from jax.experimental import pallas as pl
from jax.experimental.pallas import tpu as pltpu
from jax.sharding import PartitionSpec as P

BLOCK = 128
CHUNK = 512
MESH = pl.DeviceIdType.MESH
F32 = jnp.float32
BF16 = jnp.bfloat16


def dot(a, b):
    return jnp.dot(a, b, preferred_element_type=F32)


def dot_rows(a, b):
    return lax.dot_general(a, b, (((1,), (1,)), ((), ())), preferred_element_type=F32)


def rounded(a, b):
    return dot(a.astype(BF16), b.astype(BF16))


def local_maps(
    base, lanes, blocks, dk, dv, reset_ref, k_ref, q_ref, v_ref, beta_ref,
    a_ref, d_ref, z_ref, send_ref,
):
    def columns(h, size):
        return pl.ds(pl.multiple_of((base + h) * size, size), size)

    row = lax.broadcasted_iota(jnp.int32, (BLOCK, BLOCK), 0)
    col = lax.broadcasted_iota(jnp.int32, (BLOCK, BLOCK), 1)
    diagonal = row == col
    eye = diagonal.astype(F32)
    items = [(h, b) for b in range(blocks) for h in range(lanes)]

    ks, qs, rks, rk_rows, rqs, betas, lows, scores = [], [], [], [], [], [], [], []
    for h, b in items:
        at = slice(b * BLOCK, (b + 1) * BLOCK)
        k = k_ref[at, columns(h, dk)]
        q = q_ref[at, columns(h, dk)]
        products = dot_rows(jnp.concatenate([k, q], axis=0), k)
        gram, cross = products[:BLOCK], products[BLOCK:]
        squares = jnp.where(diagonal, gram, 0.0)
        rk = lax.rsqrt(jnp.sum(squares, axis=1, keepdims=True) + 1e-6)
        rk_row = lax.rsqrt(jnp.sum(squares, axis=0, keepdims=True) + 1e-6)
        q32 = q.astype(F32)
        rq = lax.rsqrt(jnp.sum(q32 * q32, axis=1, keepdims=True) + 1e-6)
        every = beta_ref[:, at]
        wanted = lax.broadcasted_iota(jnp.int32, every.shape, 0) == base + h
        beta_row = jnp.sum(jnp.where(wanted, every, 0.0), axis=0, keepdims=True)
        beta = jnp.sum(jnp.where(diagonal, beta_row, 0.0), axis=1, keepdims=True)
        lows.append(jnp.where(row > col, gram * (beta * rk) * rk_row, 0.0))
        scores.append(jnp.where(row >= col, cross * rq, 0.0).astype(BF16))
        ks.append(k)
        qs.append(q)
        rks.append(rk)
        rk_rows.append(rk_row)
        rqs.append(rq)
        betas.append(beta_row)

    inv = []
    for low in lows:
        pairs = jnp.where((row // 2) == (col // 2), low, 0.0)
        cut = jnp.where(((row // 4) == (col // 4)) & ((row // 2) != (col // 2)), low, 0.0)
        inner = cut - pltpu.roll(cut, BLOCK - 1, 1) * jnp.sum(pairs, axis=0, keepdims=True)
        inner = inner - pltpu.roll(inner, 1, 0) * jnp.sum(pairs, axis=1, keepdims=True)
        inv.append(eye - pairs - inner)
    n = 4
    while n < BLOCK:
        cut = ((row // (2 * n)) == (col // (2 * n))) & ((row // n) != (col // n))
        narrow = [x.astype(BF16) for x in inv]
        inner = [
            dot(jnp.where(cut, low, 0.0).astype(BF16), x).astype(BF16)
            for low, x in zip(lows, narrow)
        ]
        inv = [x - dot(y, z) for x, y, z in zip(inv, narrow, inner)]
        n *= 2

    solved = []
    for (h, b), k, x, rk, rk_row, beta in zip(items, ks, inv, rks, rk_rows, betas):
        v = v_ref[b * BLOCK:(b + 1) * BLOCK, columns(h, dv)]
        scaled = x * beta
        solved.append(
            jnp.concatenate(
                [rk * rounded(scaled * rk_row, k), rk * rounded(scaled, v)], axis=1
            ).astype(BF16)
        )
    parts = [
        dot(jnp.concatenate([k.T, score], axis=0), wu)
        for k, score, wu in zip(ks, scores, solved)
    ]

    zs = [None] * lanes
    for (h, b), q, rq, part in zip(items, qs, rqs, parts):
        kept = jnp.float32(1.0)
        for slot in range(reset_ref.shape[1]):
            kept = jnp.where(reset_ref[0, slot] == b, 0.0, kept)
        take = part[:dk, :dk]
        read = rq * q.astype(F32) - part[dk:, :dk]
        if b == 0:
            linear = kept * (eye - take)
            constant = part[:dk, dk:]
            out_linear = kept * read
            out_constant = part[dk:, dk:]
        else:
            z = zs[h] * kept
            moved = rounded(jnp.concatenate([take, read], axis=0), z)
            linear = z[:, :dk] - moved[:dk, :dk]
            constant = z[:, dk:] - moved[:dk, dk:] + part[:dk, dk:]
            out_linear = moved[dk:, :dk]
            out_constant = moved[dk:, dk:] + part[dk:, dk:]
        zs[h] = jnp.concatenate([linear, constant], axis=1)
        a_ref[base + h, b * BLOCK:(b + 1) * BLOCK] = out_linear.astype(BF16)
        d_ref[base + h, b * BLOCK:(b + 1) * BLOCK] = out_constant.astype(BF16)
    for h in range(lanes):
        z_ref[base + h] = zs[h][:, dk:]
        send_ref[base + h] = zs[h].astype(BF16)


def layer_kernel(
    shards, groups, heads, dk, dv, chunks,
    reset_ref, k_ref, q_ref, v_ref, beta_ref, w_ref, out_ref,
    a_ref, d_ref, z_ref, zb_ref,
    w_vmem, before, joined, chain, came, goes, hands, normed, give1, take1, kept, give2, take2, own,
    w_sem, pair_send, pair_recv, chain_send, chain_recv, step_send, step_recv, send1, recv1, send2, recv2,
):
    tokens = k_ref.shape[0]
    rows = tokens // groups
    pairs = groups // 2
    half = pairs * rows
    s = lax.axis_index("seq")
    g = lax.axis_index("head")
    y, c = g // 2, g % 2
    mate = y * 2 + (1 - c)

    for j in range(chunks):
        pltpu.make_async_copy(
            w_ref.at[:, pl.ds(j * CHUNK, CHUNK)], w_vmem.at[j], w_sem.at[j]
        ).start()

    share = heads // 2
    parity = s % 2
    odd = parity == 1
    partner = s + 1 - 2 * parity

    def mine(i):
        return (1 - parity) * share + i

    def theirs(i):
        return parity * share + i

    barrier = pltpu.get_barrier_semaphore()

    def greet(**place):
        pl.semaphore_signal(barrier, inc=1, device_id=place, device_id_type=MESH)

    for gap in (1, 2):
        @pl.when(s >= gap)
        def _():
            greet(seq=s - gap)

        @pl.when(s < shards - gap)
        def _():
            greet(seq=s + gap)

    greet(head=mate)
    for step in range(1, pairs):
        greet(head=((y + step) % pairs) * 2 + c)
    def to_partner(i):
        return pltpu.make_async_remote_copy(
            src_ref=zb_ref.at[theirs(i)], dst_ref=before.at[i],
            send_sem=pair_send.at[i], recv_sem=pair_recv.at[i],
            device_id={"seq": partner}, device_id_type=MESH,
        )

    def to_chain(i):
        return pltpu.make_async_remote_copy(
            src_ref=goes.at[i], dst_ref=chain.at[i],
            send_sem=chain_send.at[i], recv_sem=chain_recv.at[i],
            device_id={"seq": jnp.minimum(s + 2, shards - 1)}, device_id_type=MESH,
        )

    def to_next(i):
        return pltpu.make_async_remote_copy(
            src_ref=hands.at[i], dst_ref=came.at[i],
            send_sem=step_send.at[i], recv_sem=step_recv.at[i],
            device_id={"seq": jnp.minimum(s + 1, shards - 1)}, device_id_type=MESH,
        )

    def maps(turn, carry):
        local_maps(
            jnp.where(turn == 0, theirs(0), mine(0)), share, tokens // BLOCK, dk, dv,
            reset_ref, k_ref, q_ref, v_ref, beta_ref, a_ref, d_ref, z_ref, zb_ref,
        )

        @pl.when(turn == 0)
        def _():
            pl.semaphore_wait(
                barrier,
                pairs
                + jnp.where(s >= 1, 1, 0) + jnp.where(s >= 2, 1, 0)
                + jnp.where(s < shards - 1, 1, 0) + jnp.where(s < shards - 2, 1, 0),
            )
            for i in range(share):
                to_partner(i).start()

        return carry

    lax.fori_loop(0, 2, maps, 0)

    def replay(h, memory):
        attended = dot(a_ref[h], memory) + d_ref[h].astype(F32)
        scale = lax.rsqrt(jnp.mean(attended * attended, axis=1, keepdims=True) + 1e-5)
        result = (attended * scale).astype(BF16)
        columns = pl.ds(pl.multiple_of(h * dv, dv), dv)
        for t in range(groups):
            place = jnp.where(c == t % 2, half, 0) + (t // 2) * rows
            normed[pl.ds(pl.multiple_of(place, rows), rows), columns] = result[
                t * rows:(t + 1) * rows
            ]

    for i in range(share):
        h = mine(i)
        to_partner(i).wait_recv()

        @pl.when(odd)
        def _():
            both = dot(zb_ref[h, :, :dk], before[i])
            joined[i, :, :dk] = both[:, :dk]
            joined[i, :, dk:] = both[:, dk:] + z_ref[h]

        @pl.when(jnp.logical_not(odd))
        def _():
            both = dot(before[i, :, :dk], zb_ref[h])
            joined[i, :, :dk] = both[:, :dk]
            joined[i, :, dk:] = both[:, dk:] + before[i, :, dk:].astype(F32)

        @pl.when(s < 2)
        def _():
            chain[i] = jnp.zeros((dk, dv), BF16)

        @pl.when(s >= 2)
        def _():
            to_chain(i).wait_recv()

        goes[i] = (
            dot(joined[i, :, :dk].astype(BF16), chain[i]) + joined[i, :, dk:]
        ).astype(BF16)

        @pl.when(s < shards - 2)
        def _():
            to_chain(i).start()

        @pl.when(odd)
        def _():
            hands[i] = goes[i]
            joined[i, :, dk:] = (
                dot(before[i, :, :dk], chain[i]) + before[i, :, dk:].astype(F32)
            )

        @pl.when(jnp.logical_not(odd))
        def _():
            hands[i] = (dot(zb_ref[h, :, :dk], chain[i]) + z_ref[h]).astype(BF16)
            joined[i, :, dk:] = chain[i].astype(F32)

        @pl.when(s < shards - 1)
        def _():
            to_next(i).start()

    for i in range(share):
        replay(mine(i), joined[i, :, dk:].astype(BF16))

    for i in range(share):
        @pl.when(s == 0)
        def _():
            came[i] = jnp.zeros((dk, dv), BF16)

        @pl.when(s > 0)
        def _():
            to_next(i).wait_recv()

        replay(theirs(i), came[i])

    def first(j):
        return pltpu.make_async_remote_copy(
            src_ref=give1.at[j], dst_ref=take1.at[j],
            send_sem=send1.at[j], recv_sem=recv1.at[j],
            device_id={"head": mate}, device_id_type=MESH,
        )

    def second(j, step):
        other = (y + step) % pairs
        return pltpu.make_async_remote_copy(
            src_ref=give2.at[j, step - 1], dst_ref=take2.at[j, step - 1],
            send_sem=send2.at[j, step - 1], recv_sem=recv2.at[j, step - 1],
            device_id={"head": other * 2 + c}, device_id_type=MESH,
        )

    def pass_on(j):
        first(j).wait_recv()
        for step in range(1, pairs):
            at = pl.ds(pl.multiple_of(((y + step) % pairs) * rows, rows), rows)
            give2[j, step - 1] = (kept[j, at] + take1[j, at].astype(F32)).astype(BF16)
            second(j, step).start()
        at = pl.ds(pl.multiple_of(y * rows, rows), rows)
        own[j] = kept[j, at] + take1[j, at].astype(F32)

    def project(j, carry):
        pltpu.make_async_copy(
            w_ref.at[:, pl.ds(j * CHUNK, CHUNK)], w_vmem.at[j], w_sem.at[j]
        ).wait()
        part = dot(normed[...], w_vmem[j])
        give1[j] = part[:half].astype(BF16)
        first(j).start()
        kept[j] = part[half:]

        @pl.when(j > 0)
        def _():
            pass_on(j - 1)

        return carry

    lax.fori_loop(0, chunks, project, 0)
    pass_on(chunks - 1)

    for j in range(chunks):
        total = own[j]
        for step in range(1, pairs):
            second(j, step).wait_recv()
            total = total + take2[j, step - 1].astype(F32)
        out_ref[:, j * CHUNK:(j + 1) * CHUNK] = total.astype(BF16)

    for j in range(chunks):
        first(j).wait_send()
        for step in range(1, pairs):
            second(j, step).wait_send()

    for i in range(share):
        to_partner(i).wait_send()

    @pl.when(s < shards - 2)
    def _():
        for i in range(share):
            to_chain(i).wait_send()

    @pl.when(s < shards - 1)
    def _():
        for i in range(share):
            to_next(i).wait_send()


def layer(resets, k, q, v, beta, w, shards, groups, heads, dk, dv):
    tokens = k.shape[0]
    width = w.shape[1]
    chunks = width // CHUNK
    rows = tokens // groups
    pairs = groups // 2
    half = pairs * rows
    far = max(pairs - 1, 1)
    share = heads // 2
    vmem = pl.BlockSpec(memory_space=pltpu.VMEM)
    dma = pltpu.SemaphoreType.DMA
    return pl.pallas_call(
        functools.partial(layer_kernel, shards, groups, heads, dk, dv, chunks),
        in_specs=[
            pl.BlockSpec(memory_space=pltpu.SMEM), vmem, vmem, vmem, vmem,
            pl.BlockSpec(memory_space=pl.ANY),
        ],
        out_specs=vmem,
        out_shape=jax.ShapeDtypeStruct((rows, width), BF16),
        scratch_shapes=[
            pltpu.VMEM((heads, tokens, dk), BF16),
            pltpu.VMEM((heads, tokens, dv), BF16),
            pltpu.VMEM((heads, dk, dv), F32),
            pltpu.VMEM((heads, dk, dk + dv), BF16),
            pltpu.VMEM((chunks, w.shape[0], CHUNK), BF16),
            pltpu.VMEM((share, dk, dk + dv), BF16),
            pltpu.VMEM((share, dk, dk + dv), F32),
            pltpu.VMEM((share, dk, dv), BF16),
            pltpu.VMEM((share, dk, dv), BF16),
            pltpu.VMEM((share, dk, dv), BF16),
            pltpu.VMEM((share, dk, dv), BF16),
            pltpu.VMEM((tokens, heads * dv), BF16),
            pltpu.VMEM((chunks, half, CHUNK), BF16),
            pltpu.VMEM((chunks, half, CHUNK), BF16),
            pltpu.VMEM((chunks, half, CHUNK), F32),
            pltpu.VMEM((chunks, far, rows, CHUNK), BF16),
            pltpu.VMEM((chunks, far, rows, CHUNK), BF16),
            pltpu.VMEM((chunks, rows, CHUNK), F32),
            dma((chunks,)),
            dma((share,)),
            dma((share,)),
            dma((share,)),
            dma((share,)),
            dma((share,)),
            dma((share,)),
            dma((chunks,)),
            dma((chunks,)),
            dma((chunks, far)),
            dma((chunks, far)),
        ],
        compiler_params=pltpu.CompilerParams(
            collective_id=0, has_side_effects=True, vmem_limit_bytes=56 * 1024 * 1024
        ),
        name="layer",
    )(resets, k, q, v, beta, w)


def body(shards, groups, queries, keys, values, beta, reset_blocks, out_weight):
    tokens, heads, dk = queries.shape
    dv = values.shape[2]
    return layer(
        reset_blocks,
        keys.reshape(tokens, heads * dk),
        queries.reshape(tokens, heads * dk),
        values.reshape(tokens, heads * dv),
        beta,
        out_weight,
        shards, groups, heads, dk, dv,
    )


def solution(mesh):
    return jax.shard_map(
        functools.partial(body, mesh.shape["seq"], mesh.shape["head"]),
        mesh=mesh,
        in_specs=(
            P("seq", "head", None),
            P("seq", "head", None),
            P("seq", "head", None),
            P("head", "seq"),
            P("seq", None),
            P("head", None),
        ),
        out_specs=P(("seq", "head"), None),
        check_vma=False,
    )
```

```python
import functools

import jax
import jax.numpy as jnp
from jax import lax
from jax.experimental import pallas as pl
from jax.experimental.pallas import tpu as pltpu
from jax.sharding import PartitionSpec as P

BLOCK = 128
CHUNK = 256
MESH = pl.DeviceIdType.MESH
F32 = jnp.float32
BF16 = jnp.bfloat16


def dot(a, b):
    return jnp.dot(a, b, preferred_element_type=F32)


def dot_rows(a, b):
    return lax.dot_general(a, b, (((1,), (1,)), ((), ())), preferred_element_type=F32)


def rounded(a, b):
    return dot(a.astype(BF16), b.astype(BF16))


def even_blocks(x, n):
    return jnp.concatenate([x[i:i + n] for i in range(0, x.shape[0], 2 * n)], axis=0)


def odd_blocks(x, n):
    return jnp.concatenate([x[i:i + n] for i in range(n, x.shape[0], 2 * n)], axis=0)


def interleave(even, odd, n):
    rows = []
    for i in range(0, even.shape[0], n):
        rows += [even[i:i + n], odd[i:i + n]]
    return jnp.concatenate(rows, axis=0)


def local_maps(
    base, lanes, blocks, dk, dv, reset_ref, k_ref, q_ref, v_ref, beta_ref,
    a_ref, d_ref, z_ref, send_ref,
):
    def columns(h, size):
        return pl.ds(pl.multiple_of((base + h) * size, size), size)

    row = lax.broadcasted_iota(jnp.int32, (BLOCK, BLOCK), 0)
    col = lax.broadcasted_iota(jnp.int32, (BLOCK, BLOCK), 1)
    diagonal = row == col
    eye = diagonal.astype(F32)
    items = [(h, b) for b in range(blocks) for h in range(lanes)]

    ks, qs, rks, rk_rows, rqs, betas, lows, scores = [], [], [], [], [], [], [], []
    for h, b in items:
        at = slice(b * BLOCK, (b + 1) * BLOCK)
        k = k_ref[at, columns(h, dk)]
        q = q_ref[at, columns(h, dk)]
        products = dot_rows(jnp.concatenate([k, q], axis=0), k)
        gram, cross = products[:BLOCK], products[BLOCK:]
        squares = jnp.where(diagonal, gram, 0.0)
        rk = lax.rsqrt(jnp.sum(squares, axis=1, keepdims=True) + 1e-6)
        rk_row = lax.rsqrt(jnp.sum(squares, axis=0, keepdims=True) + 1e-6)
        q32 = q.astype(F32)
        rq = lax.rsqrt(jnp.sum(q32 * q32, axis=1, keepdims=True) + 1e-6)
        every = beta_ref[:, at]
        wanted = lax.broadcasted_iota(jnp.int32, every.shape, 0) == base + h
        beta_row = jnp.sum(jnp.where(wanted, every, 0.0), axis=0, keepdims=True)
        beta = jnp.sum(jnp.where(diagonal, beta_row, 0.0), axis=1, keepdims=True)
        lows.append(jnp.where(row > col, gram * (beta * rk) * rk_row, 0.0))
        scores.append(jnp.where(row >= col, cross * rq, 0.0).astype(BF16))
        ks.append(k)
        qs.append(q)
        rks.append(rk)
        rk_rows.append(rk_row)
        rqs.append(rq)
        betas.append(beta_row)

    inv = []
    for low in lows:
        pairs = jnp.where((row // 2) == (col // 2), low, 0.0)
        cut = jnp.where(((row // 4) == (col // 4)) & ((row // 2) != (col // 2)), low, 0.0)
        inner = cut - pltpu.roll(cut, BLOCK - 1, 1) * jnp.sum(pairs, axis=0, keepdims=True)
        inner = inner - pltpu.roll(inner, 1, 0) * jnp.sum(pairs, axis=1, keepdims=True)
        inv.append(eye - pairs - inner)
    narrow = [x.astype(BF16) for x in inv]
    lows = [low.astype(BF16) for low in lows]
    n = 4
    while n < BLOCK:
        cut = ((row // (2 * n)) == (col // (2 * n))) & ((row // n) != (col // n))
        cut = jnp.where(cut, 1.0, 0.0).astype(BF16)
        if n < 16:
            inner = [dot(low * cut, x).astype(BF16) for low, x in zip(lows, narrow)]
            inv = [x - dot(y, z) for x, y, z in zip(inv, narrow, inner)]
            narrow = [x.astype(BF16) for x in inv]
        else:
            below = odd_blocks(cut, n)
            inner = [
                dot(odd_blocks(low, n) * below, x).astype(BF16) for low, x in zip(lows, narrow)
            ]
            inner = [interleave(jnp.zeros_like(x), x, n) for x in inner]
            changed = [
                odd_blocks(x, n) - dot(odd_blocks(y, n), z)
                for x, y, z in zip(inv, narrow, inner)
            ]
            inv = [interleave(even_blocks(x, n), y, n) for x, y in zip(inv, changed)]
            narrow = [
                interleave(even_blocks(x, n), y.astype(BF16), n) for x, y in zip(narrow, changed)
            ]
        n *= 2

    solved = []
    for (h, b), k, x, rk, rk_row, beta in zip(items, ks, inv, rks, rk_rows, betas):
        v = v_ref[b * BLOCK:(b + 1) * BLOCK, columns(h, dv)]
        scaled = x * beta
        solved.append(
            jnp.concatenate(
                [rk * rounded(scaled * rk_row, k), rk * rounded(scaled, v)], axis=1
            ).astype(BF16)
        )
    parts = [
        dot(jnp.concatenate([k.T, score], axis=0), wu)
        for k, score, wu in zip(ks, scores, solved)
    ]

    zs = [None] * lanes
    for (h, b), q, rq, part in zip(items, qs, rqs, parts):
        kept = jnp.float32(1.0)
        for slot in range(reset_ref.shape[1]):
            kept = jnp.where(reset_ref[0, slot] == b, 0.0, kept)
        take = part[:dk, :dk]
        read = rq * q.astype(F32) - part[dk:, :dk]
        if b == 0:
            linear = kept * (eye - take)
            constant = part[:dk, dk:]
            out_linear = kept * read
            out_constant = part[dk:, dk:]
        else:
            z = zs[h] * kept
            moved = rounded(jnp.concatenate([take, read], axis=0), z)
            linear = z[:, :dk] - moved[:dk, :dk]
            constant = z[:, dk:] - moved[:dk, dk:] + part[:dk, dk:]
            out_linear = moved[dk:, :dk]
            out_constant = moved[dk:, dk:] + part[dk:, dk:]
        zs[h] = jnp.concatenate([linear, constant], axis=1)
        a_ref[base + h, b * BLOCK:(b + 1) * BLOCK] = out_linear.astype(BF16)
        d_ref[base + h, b * BLOCK:(b + 1) * BLOCK] = out_constant.astype(BF16)
    for h in range(lanes):
        z_ref[base + h] = zs[h][:, dk:]
        send_ref[base + h] = zs[h].astype(BF16)


def layer_kernel(
    shards, groups, heads, dk, dv, chunks,
    reset_ref, k_ref, q_ref, v_ref, beta_ref, w_ref, out_ref,
    a_ref, d_ref, z_ref, zb_ref,
    w_vmem, before, joined, chain, came, goes, hands, normed, give1, take1, kept, give2, take2, own,
    w_sem, pair_send, pair_recv, chain_send, chain_recv, step_send, step_recv, send1, recv1, send2, recv2,
):
    tokens = k_ref.shape[0]
    rows = tokens // groups
    pairs = groups // 2
    half = pairs * rows
    s = lax.axis_index("seq")
    g = lax.axis_index("head")
    y, c = g // 2, g % 2
    mate = y * 2 + (1 - c)

    for j in range(chunks):
        pltpu.make_async_copy(
            w_ref.at[:, pl.ds(j * CHUNK, CHUNK)], w_vmem.at[j], w_sem.at[j]
        ).start()

    share = heads // 2
    parity = s % 2
    odd = parity == 1
    partner = s + 1 - 2 * parity

    def mine(i):
        return (1 - parity) * share + i

    def theirs(i):
        return parity * share + i

    barrier = pltpu.get_barrier_semaphore()

    def greet(**place):
        pl.semaphore_signal(barrier, inc=1, device_id=place, device_id_type=MESH)

    for gap in (1, 2):
        @pl.when(s >= gap)
        def _():
            greet(seq=s - gap)

        @pl.when(s < shards - gap)
        def _():
            greet(seq=s + gap)

    greet(head=mate)
    for step in range(1, pairs):
        greet(head=((y + step) % pairs) * 2 + c)
    def to_partner(i):
        return pltpu.make_async_remote_copy(
            src_ref=zb_ref.at[theirs(i)], dst_ref=before.at[i],
            send_sem=pair_send.at[i], recv_sem=pair_recv.at[i],
            device_id={"seq": partner}, device_id_type=MESH,
        )

    def to_chain(i):
        return pltpu.make_async_remote_copy(
            src_ref=goes.at[i], dst_ref=chain.at[i],
            send_sem=chain_send.at[i], recv_sem=chain_recv.at[i],
            device_id={"seq": jnp.minimum(s + 2, shards - 1)}, device_id_type=MESH,
        )

    def to_next(i):
        return pltpu.make_async_remote_copy(
            src_ref=hands.at[i], dst_ref=came.at[i],
            send_sem=step_send.at[i], recv_sem=step_recv.at[i],
            device_id={"seq": jnp.minimum(s + 1, shards - 1)}, device_id_type=MESH,
        )

    def maps(turn, carry):
        local_maps(
            jnp.where(turn == 0, theirs(0), mine(0)), share, tokens // BLOCK, dk, dv,
            reset_ref, k_ref, q_ref, v_ref, beta_ref, a_ref, d_ref, z_ref, zb_ref,
        )

        @pl.when(turn == 0)
        def _():
            pl.semaphore_wait(
                barrier,
                pairs
                + jnp.where(s >= 1, 1, 0) + jnp.where(s >= 2, 1, 0)
                + jnp.where(s < shards - 1, 1, 0) + jnp.where(s < shards - 2, 1, 0),
            )
            for i in range(share):
                to_partner(i).start()

        return carry

    lax.fori_loop(0, 2, maps, 0)

    def replay(h, memory):
        attended = dot(a_ref[h], memory) + d_ref[h].astype(F32)
        scale = lax.rsqrt(jnp.mean(attended * attended, axis=1, keepdims=True) + 1e-5)
        result = (attended * scale).astype(BF16)
        columns = pl.ds(pl.multiple_of(h * dv, dv), dv)
        for t in range(groups):
            place = jnp.where(c == t % 2, half, 0) + (t // 2) * rows
            normed[pl.ds(pl.multiple_of(place, rows), rows), columns] = result[
                t * rows:(t + 1) * rows
            ]

    for i in range(share):
        h = mine(i)
        to_partner(i).wait_recv()

        @pl.when(odd)
        def _():
            both = dot(zb_ref[h, :, :dk], before[i])
            joined[i, :, :dk] = both[:, :dk]
            joined[i, :, dk:] = both[:, dk:] + z_ref[h]

        @pl.when(jnp.logical_not(odd))
        def _():
            both = dot(before[i, :, :dk], zb_ref[h])
            joined[i, :, :dk] = both[:, :dk]
            joined[i, :, dk:] = both[:, dk:] + before[i, :, dk:].astype(F32)

        @pl.when(s < 2)
        def _():
            chain[i] = jnp.zeros((dk, dv), BF16)

        @pl.when(s >= 2)
        def _():
            to_chain(i).wait_recv()

        goes[i] = (
            dot(joined[i, :, :dk].astype(BF16), chain[i]) + joined[i, :, dk:]
        ).astype(BF16)

        @pl.when(s < shards - 2)
        def _():
            to_chain(i).start()

        @pl.when(odd)
        def _():
            hands[i] = goes[i]
            joined[i, :, dk:] = (
                dot(before[i, :, :dk], chain[i]) + before[i, :, dk:].astype(F32)
            )

        @pl.when(jnp.logical_not(odd))
        def _():
            hands[i] = (dot(zb_ref[h, :, :dk], chain[i]) + z_ref[h]).astype(BF16)
            joined[i, :, dk:] = chain[i].astype(F32)

        @pl.when(s < shards - 1)
        def _():
            to_next(i).start()

    for i in range(share):
        replay(mine(i), joined[i, :, dk:].astype(BF16))

    for i in range(share):
        @pl.when(s == 0)
        def _():
            came[i] = jnp.zeros((dk, dv), BF16)

        @pl.when(s > 0)
        def _():
            to_next(i).wait_recv()

        replay(theirs(i), came[i])

    def first(j):
        return pltpu.make_async_remote_copy(
            src_ref=give1.at[j], dst_ref=take1.at[j],
            send_sem=send1.at[j], recv_sem=recv1.at[j],
            device_id={"head": mate}, device_id_type=MESH,
        )

    def second(j, step):
        other = (y + step) % pairs
        return pltpu.make_async_remote_copy(
            src_ref=give2.at[j, step - 1], dst_ref=take2.at[j, step - 1],
            send_sem=send2.at[j, step - 1], recv_sem=recv2.at[j, step - 1],
            device_id={"head": other * 2 + c}, device_id_type=MESH,
        )

    def pass_on(j):
        first(j).wait_recv()
        for step in range(1, pairs):
            at = pl.ds(pl.multiple_of(((y + step) % pairs) * rows, rows), rows)
            give2[j, step - 1] = (kept[j, at] + take1[j, at].astype(F32)).astype(BF16)
            second(j, step).start()
        at = pl.ds(pl.multiple_of(y * rows, rows), rows)
        own[j] = kept[j, at] + take1[j, at].astype(F32)

    def project(j, carry):
        pltpu.make_async_copy(
            w_ref.at[:, pl.ds(j * CHUNK, CHUNK)], w_vmem.at[j], w_sem.at[j]
        ).wait()
        part = dot(normed[...], w_vmem[j])
        give1[j] = part[:half].astype(BF16)
        first(j).start()
        kept[j] = part[half:]

        @pl.when(j > 0)
        def _():
            pass_on(j - 1)

        return carry

    lax.fori_loop(0, chunks, project, 0)
    pass_on(chunks - 1)

    for j in range(chunks):
        total = own[j]
        for step in range(1, pairs):
            second(j, step).wait_recv()
            total = total + take2[j, step - 1].astype(F32)
        out_ref[:, j * CHUNK:(j + 1) * CHUNK] = total.astype(BF16)

    for j in range(chunks):
        first(j).wait_send()
        for step in range(1, pairs):
            second(j, step).wait_send()

    for i in range(share):
        to_partner(i).wait_send()

    @pl.when(s < shards - 2)
    def _():
        for i in range(share):
            to_chain(i).wait_send()

    @pl.when(s < shards - 1)
    def _():
        for i in range(share):
            to_next(i).wait_send()


def layer(resets, k, q, v, beta, w, shards, groups, heads, dk, dv):
    tokens = k.shape[0]
    width = w.shape[1]
    chunks = width // CHUNK
    rows = tokens // groups
    pairs = groups // 2
    half = pairs * rows
    far = max(pairs - 1, 1)
    share = heads // 2
    vmem = pl.BlockSpec(memory_space=pltpu.VMEM)
    dma = pltpu.SemaphoreType.DMA
    return pl.pallas_call(
        functools.partial(layer_kernel, shards, groups, heads, dk, dv, chunks),
        in_specs=[
            pl.BlockSpec(memory_space=pltpu.SMEM), vmem, vmem, vmem, vmem,
            pl.BlockSpec(memory_space=pl.ANY),
        ],
        out_specs=vmem,
        out_shape=jax.ShapeDtypeStruct((rows, width), BF16),
        scratch_shapes=[
            pltpu.VMEM((heads, tokens, dk), BF16),
            pltpu.VMEM((heads, tokens, dv), BF16),
            pltpu.VMEM((heads, dk, dv), F32),
            pltpu.VMEM((heads, dk, dk + dv), BF16),
            pltpu.VMEM((chunks, w.shape[0], CHUNK), BF16),
            pltpu.VMEM((share, dk, dk + dv), BF16),
            pltpu.VMEM((share, dk, dk + dv), F32),
            pltpu.VMEM((share, dk, dv), BF16),
            pltpu.VMEM((share, dk, dv), BF16),
            pltpu.VMEM((share, dk, dv), BF16),
            pltpu.VMEM((share, dk, dv), BF16),
            pltpu.VMEM((tokens, heads * dv), BF16),
            pltpu.VMEM((chunks, half, CHUNK), BF16),
            pltpu.VMEM((chunks, half, CHUNK), BF16),
            pltpu.VMEM((chunks, half, CHUNK), F32),
            pltpu.VMEM((chunks, far, rows, CHUNK), BF16),
            pltpu.VMEM((chunks, far, rows, CHUNK), BF16),
            pltpu.VMEM((chunks, rows, CHUNK), F32),
            dma((chunks,)),
            dma((share,)),
            dma((share,)),
            dma((share,)),
            dma((share,)),
            dma((share,)),
            dma((share,)),
            dma((chunks,)),
            dma((chunks,)),
            dma((chunks, far)),
            dma((chunks, far)),
        ],
        compiler_params=pltpu.CompilerParams(
            collective_id=0, has_side_effects=True, vmem_limit_bytes=36 * 1024 * 1024
        ),
        name="layer",
    )(resets, k, q, v, beta, w)


def body(shards, groups, queries, keys, values, beta, reset_blocks, out_weight):
    tokens, heads, dk = queries.shape
    dv = values.shape[2]
    return layer(
        reset_blocks,
        keys.reshape(tokens, heads * dk),
        queries.reshape(tokens, heads * dk),
        values.reshape(tokens, heads * dv),
        beta,
        out_weight,
        shards, groups, heads, dk, dv,
    )


def solution(mesh):
    return jax.shard_map(
        functools.partial(body, mesh.shape["seq"], mesh.shape["head"]),
        mesh=mesh,
        in_specs=(
            P("seq", "head", None),
            P("seq", "head", None),
            P("seq", "head", None),
            P("head", "seq"),
            P("seq", None),
            P("head", None),
        ),
        out_specs=P(("seq", "head"), None),
        check_vma=False,
    )
```

```python
import functools

import jax
import jax.numpy as jnp
from jax import lax
from jax.experimental import pallas as pl
from jax.experimental.pallas import tpu as pltpu
from jax.sharding import PartitionSpec as P

BLOCK = 128
CHUNK = 256
LANES = 128
MESH = pl.DeviceIdType.MESH
F32 = jnp.float32
BF16 = jnp.bfloat16


def dot(a, b):
    return jnp.dot(a, b, preferred_element_type=F32)


def dot_rows(a, b):
    return lax.dot_general(a, b, (((1,), (1,)), ((), ())), preferred_element_type=F32)


def rounded(a, b):
    return dot(a.astype(BF16), b.astype(BF16))


def even_blocks(x, n):
    return jnp.concatenate([x[i:i + n] for i in range(0, x.shape[0], 2 * n)], axis=0)


def odd_blocks(x, n):
    return jnp.concatenate([x[i:i + n] for i in range(n, x.shape[0], 2 * n)], axis=0)


def interleave(even, odd, n):
    rows = []
    for i in range(0, even.shape[0], n):
        rows += [even[i:i + n], odd[i:i + n]]
    return jnp.concatenate(rows, axis=0)


def local_maps(
    base, lanes, blocks, dk, dv, reset_ref, k_ref, q_ref, v_ref, beta_ref,
    a_ref, d_ref, z_ref, send_ref,
):
    def take(ref, b, h, every):
        return ref[pl.ds(b * BLOCK * every + h, BLOCK, stride=every), :]

    heads = beta_ref.shape[0]
    row = lax.broadcasted_iota(jnp.int32, (BLOCK, BLOCK), 0)
    col = lax.broadcasted_iota(jnp.int32, (BLOCK, BLOCK), 1)
    diagonal = row == col
    eye = diagonal.astype(F32)
    items = [(h, b) for b in range(blocks) for h in range(lanes)]

    ks, qs, rks, rk_rows, rqs, betas, lows, scores = [], [], [], [], [], [], [], []
    for h, b in items:
        at = slice(b * BLOCK, (b + 1) * BLOCK)
        k = take(k_ref, b, base + h, heads).astype(BF16)
        q32 = take(q_ref, b, base + h, heads)
        q = q32.astype(BF16)
        products = dot_rows(jnp.concatenate([k, q], axis=0), k)
        gram, cross = products[:BLOCK], products[BLOCK:]
        squares = jnp.where(diagonal, gram, 0.0)
        rk = lax.rsqrt(jnp.sum(squares, axis=1, keepdims=True) + 1e-6)
        rk_row = lax.rsqrt(jnp.sum(squares, axis=0, keepdims=True) + 1e-6)
        rq = lax.rsqrt(jnp.sum(q32 * q32, axis=1, keepdims=True) + 1e-6)
        every = beta_ref[:, at]
        wanted = lax.broadcasted_iota(jnp.int32, every.shape, 0) == base + h
        beta_row = jnp.sum(jnp.where(wanted, every, 0.0), axis=0, keepdims=True)
        beta = jnp.sum(jnp.where(diagonal, beta_row, 0.0), axis=1, keepdims=True)
        lows.append(jnp.where(row > col, gram * (beta * rk) * rk_row, 0.0))
        scores.append(jnp.where(row >= col, cross * rq, 0.0).astype(BF16))
        ks.append(k)
        qs.append(q)
        rks.append(rk)
        rk_rows.append(rk_row)
        rqs.append(rq)
        betas.append(beta_row)

    inv = []
    for low in lows:
        pairs = jnp.where((row // 2) == (col // 2), low, 0.0)
        cut = jnp.where(((row // 4) == (col // 4)) & ((row // 2) != (col // 2)), low, 0.0)
        inner = cut - pltpu.roll(cut, BLOCK - 1, 1) * jnp.sum(pairs, axis=0, keepdims=True)
        inner = inner - pltpu.roll(inner, 1, 0) * jnp.sum(pairs, axis=1, keepdims=True)
        inv.append(eye - pairs - inner)
    narrow = [x.astype(BF16) for x in inv]
    lows = [low.astype(BF16) for low in lows]
    n = 4
    while n < BLOCK:
        cut = ((row // (2 * n)) == (col // (2 * n))) & ((row // n) != (col // n))
        cut = jnp.where(cut, 1.0, 0.0).astype(BF16)
        if n < 16:
            inner = [dot(low * cut, x).astype(BF16) for low, x in zip(lows, narrow)]
            inv = [x - dot(y, z) for x, y, z in zip(inv, narrow, inner)]
            narrow = [x.astype(BF16) for x in inv]
        else:
            below = odd_blocks(cut, n)
            inner = [
                dot(odd_blocks(low, n) * below, x).astype(BF16) for low, x in zip(lows, narrow)
            ]
            inner = [interleave(jnp.zeros_like(x), x, n) for x in inner]
            changed = [
                odd_blocks(x, n) - dot(odd_blocks(y, n), z)
                for x, y, z in zip(inv, narrow, inner)
            ]
            inv = [interleave(even_blocks(x, n), y, n) for x, y in zip(inv, changed)]
            narrow = [
                interleave(even_blocks(x, n), y.astype(BF16), n) for x, y in zip(narrow, changed)
            ]
        n *= 2

    solved = []
    for (h, b), k, x, rk, rk_row, beta in zip(items, ks, inv, rks, rk_rows, betas):
        pieces = dv // LANES
        v = jnp.concatenate(
            [take(v_ref, b, base + h + heads * i, heads * pieces) for i in range(pieces)], axis=1
        )
        scaled = x * beta
        solved.append(
            jnp.concatenate(
                [rk * rounded(scaled * rk_row, k), rk * rounded(scaled, v)], axis=1
            ).astype(BF16)
        )
    parts = [
        dot(jnp.concatenate([k.T, score], axis=0), wu)
        for k, score, wu in zip(ks, scores, solved)
    ]

    zs = [None] * lanes
    for (h, b), q, rq, part in zip(items, qs, rqs, parts):
        kept = jnp.float32(1.0)
        for slot in range(reset_ref.shape[1]):
            kept = jnp.where(reset_ref[0, slot] == b, 0.0, kept)
        pull = part[:dk, :dk]
        read = rq * q.astype(F32) - part[dk:, :dk]
        if b == 0:
            linear = kept * (eye - pull)
            constant = part[:dk, dk:]
            out_linear = kept * read
            out_constant = part[dk:, dk:]
        else:
            z = zs[h] * kept
            moved = rounded(jnp.concatenate([pull, read], axis=0), z)
            linear = z[:, :dk] - moved[:dk, :dk]
            constant = z[:, dk:] - moved[:dk, dk:] + part[:dk, dk:]
            out_linear = moved[dk:, :dk]
            out_constant = moved[dk:, dk:] + part[dk:, dk:]
        zs[h] = jnp.concatenate([linear, constant], axis=1)
        a_ref[base + h, b * BLOCK:(b + 1) * BLOCK] = out_linear.astype(BF16)
        d_ref[base + h, b * BLOCK:(b + 1) * BLOCK] = out_constant.astype(BF16)
    for h in range(lanes):
        z_ref[base + h] = zs[h][:, dk:]
        send_ref[base + h] = zs[h].astype(BF16)


def layer_kernel(
    shards, groups, heads, dk, dv, chunks,
    reset_hbm, k_rows, q_rows, v_rows, beta_hbm, w_ref, out_ref,
    k_ref, q_ref, v_ref, reset_ref, beta_ref, a_ref, d_ref, z_ref, zb_ref,
    w_vmem, before, joined, chain, came, goes, hands, normed, give1, take1, kept, give2, take2, own,
    small_sem, w_sem, pair_send, pair_recv, chain_send, chain_recv, step_send, step_recv, send1, recv1, send2, recv2,
):
    tokens = beta_hbm.shape[1]
    rows = tokens // groups
    pairs = groups // 2
    half = pairs * rows
    s = lax.axis_index("seq")
    g = lax.axis_index("head")
    y, c = g // 2, g % 2
    mate = y * 2 + (1 - c)

    small = [
        pltpu.make_async_copy(beta_hbm, beta_ref, small_sem.at[0]),
        pltpu.make_async_copy(reset_hbm, reset_ref, small_sem.at[1]),
    ]
    for copy in small:
        copy.start()
    for j in range(chunks):
        pltpu.make_async_copy(
            w_ref.at[:, pl.ds(j * CHUNK, CHUNK)], w_vmem.at[j], w_sem.at[j]
        ).start()

    share = heads // 2
    parity = s % 2
    odd = parity == 1
    partner = s + 1 - 2 * parity

    def mine(i):
        return (1 - parity) * share + i

    def theirs(i):
        return parity * share + i

    barrier = pltpu.get_barrier_semaphore()

    def greet(**place):
        pl.semaphore_signal(barrier, inc=1, device_id=place, device_id_type=MESH)

    for gap in (1, 2):
        @pl.when(s >= gap)
        def _():
            greet(seq=s - gap)

        @pl.when(s < shards - gap)
        def _():
            greet(seq=s + gap)

    greet(head=mate)
    for step in range(1, pairs):
        greet(head=((y + step) % pairs) * 2 + c)
    def to_partner(i):
        return pltpu.make_async_remote_copy(
            src_ref=zb_ref.at[theirs(i)], dst_ref=before.at[i],
            send_sem=pair_send.at[i], recv_sem=pair_recv.at[i],
            device_id={"seq": partner}, device_id_type=MESH,
        )

    def to_chain(i):
        return pltpu.make_async_remote_copy(
            src_ref=goes.at[i], dst_ref=chain.at[i],
            send_sem=chain_send.at[i], recv_sem=chain_recv.at[i],
            device_id={"seq": jnp.minimum(s + 2, shards - 1)}, device_id_type=MESH,
        )

    def to_next(i):
        return pltpu.make_async_remote_copy(
            src_ref=hands.at[i], dst_ref=came.at[i],
            send_sem=step_send.at[i], recv_sem=step_recv.at[i],
            device_id={"seq": jnp.minimum(s + 1, shards - 1)}, device_id_type=MESH,
        )

    def maps(turn, carry):
        local_maps(
            jnp.where(turn == 0, theirs(0), mine(0)), share, tokens // BLOCK, dk, dv,
            reset_ref, k_ref, q_ref, v_ref, beta_ref, a_ref, d_ref, z_ref, zb_ref,
        )

        @pl.when(turn == 0)
        def _():
            pl.semaphore_wait(
                barrier,
                pairs
                + jnp.where(s >= 1, 1, 0) + jnp.where(s >= 2, 1, 0)
                + jnp.where(s < shards - 1, 1, 0) + jnp.where(s < shards - 2, 1, 0),
            )
            for i in range(share):
                to_partner(i).start()

        return carry

    for wide, packed in ((k_ref, k_rows), (q_ref, q_rows), (v_ref, v_rows)):
        wide[...] = packed[...].astype(F32)
    for copy in small:
        copy.wait()
    lax.fori_loop(0, 2, maps, 0)

    def replay(h, memory):
        attended = dot(a_ref[h], memory) + d_ref[h].astype(F32)
        scale = lax.rsqrt(jnp.mean(attended * attended, axis=1, keepdims=True) + 1e-5)
        result = (attended * scale).astype(BF16)
        columns = pl.ds(pl.multiple_of(h * dv, dv), dv)
        for t in range(groups):
            place = jnp.where(c == t % 2, half, 0) + (t // 2) * rows
            normed[pl.ds(pl.multiple_of(place, rows), rows), columns] = result[
                t * rows:(t + 1) * rows
            ]

    for i in range(share):
        h = mine(i)
        to_partner(i).wait_recv()

        @pl.when(odd)
        def _():
            both = dot(zb_ref[h, :, :dk], before[i])
            joined[i, :, :dk] = both[:, :dk]
            joined[i, :, dk:] = both[:, dk:] + z_ref[h]

        @pl.when(jnp.logical_not(odd))
        def _():
            both = dot(before[i, :, :dk], zb_ref[h])
            joined[i, :, :dk] = both[:, :dk]
            joined[i, :, dk:] = both[:, dk:] + before[i, :, dk:].astype(F32)

        @pl.when(s < 2)
        def _():
            chain[i] = jnp.zeros((dk, dv), BF16)

        @pl.when(s >= 2)
        def _():
            to_chain(i).wait_recv()

        goes[i] = (
            dot(joined[i, :, :dk].astype(BF16), chain[i]) + joined[i, :, dk:]
        ).astype(BF16)

        @pl.when(s < shards - 2)
        def _():
            to_chain(i).start()

        @pl.when(odd)
        def _():
            hands[i] = goes[i]
            joined[i, :, dk:] = (
                dot(before[i, :, :dk], chain[i]) + before[i, :, dk:].astype(F32)
            )

        @pl.when(jnp.logical_not(odd))
        def _():
            hands[i] = (dot(zb_ref[h, :, :dk], chain[i]) + z_ref[h]).astype(BF16)
            joined[i, :, dk:] = chain[i].astype(F32)

        @pl.when(s < shards - 1)
        def _():
            to_next(i).start()

    for i in range(share):
        replay(mine(i), joined[i, :, dk:].astype(BF16))

    for i in range(share):
        @pl.when(s == 0)
        def _():
            came[i] = jnp.zeros((dk, dv), BF16)

        @pl.when(s > 0)
        def _():
            to_next(i).wait_recv()

        replay(theirs(i), came[i])

    def first(j):
        return pltpu.make_async_remote_copy(
            src_ref=give1.at[j], dst_ref=take1.at[j],
            send_sem=send1.at[j], recv_sem=recv1.at[j],
            device_id={"head": mate}, device_id_type=MESH,
        )

    def second(j, step):
        other = (y + step) % pairs
        return pltpu.make_async_remote_copy(
            src_ref=give2.at[j, step - 1], dst_ref=take2.at[j, step - 1],
            send_sem=send2.at[j, step - 1], recv_sem=recv2.at[j, step - 1],
            device_id={"head": other * 2 + c}, device_id_type=MESH,
        )

    def pass_on(j):
        first(j).wait_recv()
        for step in range(1, pairs):
            at = pl.ds(pl.multiple_of(((y + step) % pairs) * rows, rows), rows)
            give2[j, step - 1] = (kept[j, at] + take1[j, at].astype(F32)).astype(BF16)
            second(j, step).start()
        at = pl.ds(pl.multiple_of(y * rows, rows), rows)
        own[j] = kept[j, at] + take1[j, at].astype(F32)

    def project(j, carry):
        pltpu.make_async_copy(
            w_ref.at[:, pl.ds(j * CHUNK, CHUNK)], w_vmem.at[j], w_sem.at[j]
        ).wait()
        part = dot(normed[...], w_vmem[j])
        give1[j] = part[:half].astype(BF16)
        first(j).start()
        kept[j] = part[half:]

        @pl.when(j > 0)
        def _():
            pass_on(j - 1)

        return carry

    lax.fori_loop(0, chunks, project, 0)
    pass_on(chunks - 1)

    for j in range(chunks):
        total = own[j]
        for step in range(1, pairs):
            second(j, step).wait_recv()
            total = total + take2[j, step - 1].astype(F32)
        out_ref[:, j * CHUNK:(j + 1) * CHUNK] = total.astype(BF16)

    for j in range(chunks):
        first(j).wait_send()
        for step in range(1, pairs):
            second(j, step).wait_send()

    for i in range(share):
        to_partner(i).wait_send()

    @pl.when(s < shards - 2)
    def _():
        for i in range(share):
            to_chain(i).wait_send()

    @pl.when(s < shards - 1)
    def _():
        for i in range(share):
            to_next(i).wait_send()


def layer(resets, k, q, v, beta, w, shards, groups, heads, dk, dv):
    tokens = beta.shape[1]
    width = w.shape[1]
    chunks = width // CHUNK
    rows = tokens // groups
    pairs = groups // 2
    half = pairs * rows
    far = max(pairs - 1, 1)
    share = heads // 2
    vmem = pl.BlockSpec(memory_space=pltpu.VMEM)
    hbm = pl.BlockSpec(memory_space=pltpu.HBM)
    dma = pltpu.SemaphoreType.DMA
    return pl.pallas_call(
        functools.partial(layer_kernel, shards, groups, heads, dk, dv, chunks),
        in_specs=[hbm, vmem, vmem, vmem, hbm, hbm],
        out_specs=vmem,
        out_shape=jax.ShapeDtypeStruct((rows, width), BF16),
        scratch_shapes=[
            pltpu.VMEM(k.shape, F32),
            pltpu.VMEM(q.shape, F32),
            pltpu.VMEM(v.shape, F32),
            pltpu.SMEM(resets.shape, resets.dtype),
            pltpu.VMEM(beta.shape, beta.dtype),
            pltpu.VMEM((heads, tokens, dk), BF16),
            pltpu.VMEM((heads, tokens, dv), BF16),
            pltpu.VMEM((heads, dk, dv), F32),
            pltpu.VMEM((heads, dk, dk + dv), BF16),
            pltpu.VMEM((chunks, w.shape[0], CHUNK), BF16),
            pltpu.VMEM((share, dk, dk + dv), BF16),
            pltpu.VMEM((share, dk, dk + dv), F32),
            pltpu.VMEM((share, dk, dv), BF16),
            pltpu.VMEM((share, dk, dv), BF16),
            pltpu.VMEM((share, dk, dv), BF16),
            pltpu.VMEM((share, dk, dv), BF16),
            pltpu.VMEM((tokens, heads * dv), BF16),
            pltpu.VMEM((chunks, half, CHUNK), BF16),
            pltpu.VMEM((chunks, half, CHUNK), BF16),
            pltpu.VMEM((chunks, half, CHUNK), F32),
            pltpu.VMEM((chunks, far, rows, CHUNK), BF16),
            pltpu.VMEM((chunks, far, rows, CHUNK), BF16),
            pltpu.VMEM((chunks, rows, CHUNK), F32),
            dma((2,)),
            dma((chunks,)),
            dma((share,)),
            dma((share,)),
            dma((share,)),
            dma((share,)),
            dma((share,)),
            dma((share,)),
            dma((chunks,)),
            dma((chunks,)),
            dma((chunks, far)),
            dma((chunks, far)),
        ],
        compiler_params=pltpu.CompilerParams(
            collective_id=0, has_side_effects=True, vmem_limit_bytes=56 * 1024 * 1024
        ),
        name="layer",
    )(resets, k, q, v, beta, w)


def body(shards, groups, queries, keys, values, beta, reset_blocks, out_weight):
    tokens, heads, dk = queries.shape
    dv = values.shape[2]
    return layer(
        reset_blocks,
        keys.reshape(tokens * heads, dk),
        queries.reshape(tokens * heads, dk),
        values.reshape(tokens, heads, dv // LANES, LANES)
        .transpose(0, 2, 1, 3)
        .reshape(tokens * (dv // LANES) * heads, LANES),
        beta,
        out_weight,
        shards, groups, heads, dk, dv,
    )


def solution(mesh):
    return jax.shard_map(
        functools.partial(body, mesh.shape["seq"], mesh.shape["head"]),
        mesh=mesh,
        in_specs=(
            P("seq", "head", None),
            P("seq", "head", None),
            P("seq", "head", None),
            P("head", "seq"),
            P("seq", None),
            P("head", None),
        ),
        out_specs=P(("seq", "head"), None),
        check_vma=False,
    )
```

```python
import functools

import jax
import jax.numpy as jnp
from jax import lax
from jax.experimental import pallas as pl
from jax.experimental.pallas import tpu as pltpu
from jax.sharding import PartitionSpec as P

BLOCK = 128
CHUNK = 256
LANES = 128
MESH = pl.DeviceIdType.MESH
F32 = jnp.float32
BF16 = jnp.bfloat16


def dot(a, b):
    return jnp.dot(a, b, preferred_element_type=F32)


def dot_rows(a, b):
    return lax.dot_general(a, b, (((1,), (1,)), ((), ())), preferred_element_type=F32)


def rounded(a, b):
    return dot(a.astype(BF16), b.astype(BF16))


def even_blocks(x, n):
    return jnp.concatenate([x[i:i + n] for i in range(0, x.shape[0], 2 * n)], axis=0)


def odd_blocks(x, n):
    return jnp.concatenate([x[i:i + n] for i in range(n, x.shape[0], 2 * n)], axis=0)


def interleave(even, odd, n):
    rows = []
    for i in range(0, even.shape[0], n):
        rows += [even[i:i + n], odd[i:i + n]]
    return jnp.concatenate(rows, axis=0)


def local_maps(
    base, lanes, blocks, dk, dv, reset_ref, k_ref, q_ref, v_ref, beta_ref,
    a_ref, d_ref, z_ref, send_ref,
):
    def take(ref, b, h, every):
        return ref[pl.ds(b * BLOCK * every + h, BLOCK, stride=every), :]

    heads = beta_ref.shape[0]
    row = lax.broadcasted_iota(jnp.int32, (BLOCK, BLOCK), 0)
    col = lax.broadcasted_iota(jnp.int32, (BLOCK, BLOCK), 1)
    diagonal = row == col
    eye = diagonal.astype(F32)
    items = [(h, b) for b in range(blocks) for h in range(lanes)]

    ks, qs, rks, rk_rows, rqs, betas, lows, scores = [], [], [], [], [], [], [], []
    for h, b in items:
        at = slice(b * BLOCK, (b + 1) * BLOCK)
        k = take(k_ref, b, base + h, heads).astype(BF16)
        q32 = take(q_ref, b, base + h, heads)
        q = q32.astype(BF16)
        products = dot_rows(jnp.concatenate([k, q], axis=0), k)
        gram, cross = products[:BLOCK], products[BLOCK:]
        squares = jnp.where(diagonal, gram, 0.0)
        rk = lax.rsqrt(jnp.sum(squares, axis=1, keepdims=True) + 1e-6)
        rk_row = lax.rsqrt(jnp.sum(squares, axis=0, keepdims=True) + 1e-6)
        rq = lax.rsqrt(jnp.sum(q32 * q32, axis=1, keepdims=True) + 1e-6)
        every = beta_ref[:, at]
        wanted = lax.broadcasted_iota(jnp.int32, every.shape, 0) == base + h
        beta_row = jnp.sum(jnp.where(wanted, every, 0.0), axis=0, keepdims=True)
        beta = jnp.sum(jnp.where(diagonal, beta_row, 0.0), axis=1, keepdims=True)
        lows.append(jnp.where(row > col, gram * (beta * rk) * rk_row, 0.0))
        scores.append(jnp.where(row >= col, cross * rq, 0.0).astype(BF16))
        ks.append(k)
        qs.append(q)
        rks.append(rk)
        rk_rows.append(rk_row)
        rqs.append(rq)
        betas.append(beta_row)

    inv = []
    for low in lows:
        pairs = jnp.where((row // 2) == (col // 2), low, 0.0)
        cut = jnp.where(((row // 4) == (col // 4)) & ((row // 2) != (col // 2)), low, 0.0)
        inner = cut - pltpu.roll(cut, BLOCK - 1, 1) * jnp.sum(pairs, axis=0, keepdims=True)
        inner = inner - pltpu.roll(inner, 1, 0) * jnp.sum(pairs, axis=1, keepdims=True)
        inv.append(eye - pairs - inner)
    narrow = [x.astype(BF16) for x in inv]
    lows = [low.astype(BF16) for low in lows]
    n = 4
    while n < BLOCK:
        cut = ((row // (2 * n)) == (col // (2 * n))) & ((row // n) != (col // n))
        cut = jnp.where(cut, 1.0, 0.0).astype(BF16)
        if n < 16:
            inner = [dot(low * cut, x).astype(BF16) for low, x in zip(lows, narrow)]
            inv = [x - dot(y, z) for x, y, z in zip(inv, narrow, inner)]
            narrow = [x.astype(BF16) for x in inv]
        else:
            below = odd_blocks(cut, n)
            inner = [
                dot(odd_blocks(low, n) * below, x).astype(BF16) for low, x in zip(lows, narrow)
            ]
            inner = [interleave(jnp.zeros_like(x), x, n) for x in inner]
            changed = [
                odd_blocks(x, n) - dot(odd_blocks(y, n), z)
                for x, y, z in zip(inv, narrow, inner)
            ]
            inv = [interleave(even_blocks(x, n), y, n) for x, y in zip(inv, changed)]
            narrow = [
                interleave(even_blocks(x, n), y.astype(BF16), n) for x, y in zip(narrow, changed)
            ]
        n *= 2

    solved = []
    for (h, b), k, x, rk, rk_row, beta in zip(items, ks, inv, rks, rk_rows, betas):
        pieces = dv // LANES
        v = jnp.concatenate(
            [take(v_ref, b, base + h + heads * i, heads * pieces) for i in range(pieces)], axis=1
        )
        scaled = x * beta
        solved.append(
            jnp.concatenate(
                [rk * rounded(scaled * rk_row, k), rk * rounded(scaled, v)], axis=1
            ).astype(BF16)
        )
    parts = [
        dot(jnp.concatenate([k.T, score], axis=0), wu)
        for k, score, wu in zip(ks, scores, solved)
    ]

    zs = [None] * lanes
    for (h, b), q, rq, part in zip(items, qs, rqs, parts):
        kept = jnp.float32(1.0)
        for slot in range(reset_ref.shape[1]):
            kept = jnp.where(reset_ref[0, slot] == b, 0.0, kept)
        pull = part[:dk, :dk]
        read = rq * q.astype(F32) - part[dk:, :dk]
        if b == 0:
            linear = kept * (eye - pull)
            constant = part[:dk, dk:]
            out_linear = kept * read
            out_constant = part[dk:, dk:]
        else:
            z = zs[h] * kept
            moved = rounded(jnp.concatenate([pull, read], axis=0), z)
            linear = z[:, :dk] - moved[:dk, :dk]
            constant = z[:, dk:] - moved[:dk, dk:] + part[:dk, dk:]
            out_linear = moved[dk:, :dk]
            out_constant = moved[dk:, dk:] + part[dk:, dk:]
        zs[h] = jnp.concatenate([linear, constant], axis=1)
        a_ref[base + h, b * BLOCK:(b + 1) * BLOCK] = out_linear.astype(BF16)
        d_ref[base + h, b * BLOCK:(b + 1) * BLOCK] = out_constant.astype(BF16)
    for h in range(lanes):
        z_ref[base + h] = zs[h][:, dk:]
        send_ref[base + h] = zs[h].astype(BF16)


def layer_kernel(
    shards, groups, heads, dk, dv, chunks,
    reset_hbm, k_rows, q_rows, v_rows, beta_hbm, w_ref, out_ref,
    k_ref, q_ref, v_ref, reset_ref, beta_ref, a_ref, d_ref, z_ref, zb_ref,
    w_vmem, before, joined, chain, came, goes, hands, normed, give1, take1, kept, give2, take2, own,
    small_sem, w_sem, pair_send, pair_recv, chain_send, chain_recv, step_send, step_recv, send1, recv1, send2, recv2,
):
    tokens = beta_hbm.shape[1]
    rows = tokens // groups
    pairs = groups // 2
    half = pairs * rows
    s = lax.axis_index("seq")
    g = lax.axis_index("head")
    y, c = g // 2, g % 2
    mate = y * 2 + (1 - c)

    small = [
        pltpu.make_async_copy(beta_hbm, beta_ref, small_sem.at[0]),
        pltpu.make_async_copy(reset_hbm, reset_ref, small_sem.at[1]),
    ]
    for copy in small:
        copy.start()
    for j in range(chunks):
        pltpu.make_async_copy(
            w_ref.at[:, pl.ds(j * CHUNK, CHUNK)], w_vmem.at[j], w_sem.at[j]
        ).start()

    share = heads // 2
    parity = s % 2
    odd = parity == 1
    partner = s + 1 - 2 * parity

    def mine(i):
        return (1 - parity) * share + i

    def theirs(i):
        return parity * share + i

    barrier = pltpu.get_barrier_semaphore()

    def greet(**place):
        pl.semaphore_signal(barrier, inc=1, device_id=place, device_id_type=MESH)

    for gap in (1, 2):
        @pl.when(s >= gap)
        def _():
            greet(seq=s - gap)

        @pl.when(s < shards - gap)
        def _():
            greet(seq=s + gap)

    greet(head=mate)
    for step in range(1, pairs):
        greet(head=((y + step) % pairs) * 2 + c)
    def to_partner(i):
        return pltpu.make_async_remote_copy(
            src_ref=zb_ref.at[theirs(i)], dst_ref=before.at[i],
            send_sem=pair_send.at[i], recv_sem=pair_recv.at[i],
            device_id={"seq": partner}, device_id_type=MESH,
        )

    def to_chain(i):
        return pltpu.make_async_remote_copy(
            src_ref=goes.at[i], dst_ref=chain.at[i],
            send_sem=chain_send.at[i], recv_sem=chain_recv.at[i],
            device_id={"seq": jnp.minimum(s + 2, shards - 1)}, device_id_type=MESH,
        )

    def to_next(i):
        return pltpu.make_async_remote_copy(
            src_ref=hands.at[i], dst_ref=came.at[i],
            send_sem=step_send.at[i], recv_sem=step_recv.at[i],
            device_id={"seq": jnp.minimum(s + 1, shards - 1)}, device_id_type=MESH,
        )

    def maps(turn, carry):
        local_maps(
            jnp.where(turn == 0, theirs(0), mine(0)), share, tokens // BLOCK, dk, dv,
            reset_ref, k_ref, q_ref, v_ref, beta_ref, a_ref, d_ref, z_ref, zb_ref,
        )

        @pl.when(turn == 0)
        def _():
            pl.semaphore_wait(
                barrier,
                pairs
                + jnp.where(s >= 1, 1, 0) + jnp.where(s >= 2, 1, 0)
                + jnp.where(s < shards - 1, 1, 0) + jnp.where(s < shards - 2, 1, 0),
            )
            for i in range(share):
                to_partner(i).start()

        return carry

    for wide, packed in ((k_ref, k_rows), (q_ref, q_rows), (v_ref, v_rows)):
        wide[...] = packed[...].astype(F32)
    for copy in small:
        copy.wait()
    lax.fori_loop(0, 2, maps, 0)

    def replay(h, memory):
        attended = dot(a_ref[h], memory) + d_ref[h].astype(F32)
        scale = lax.rsqrt(jnp.mean(attended * attended, axis=1, keepdims=True) + 1e-5)
        result = (attended * scale).astype(BF16)
        columns = pl.ds(pl.multiple_of(h * dv, dv), dv)
        for t in range(groups):
            place = jnp.where(c == t % 2, half, 0) + (t // 2) * rows
            normed[pl.ds(pl.multiple_of(place, rows), rows), columns] = result[
                t * rows:(t + 1) * rows
            ]

    for i in range(share):
        h = mine(i)
        to_partner(i).wait_recv()

        @pl.when(odd)
        def _():
            both = dot(zb_ref[h, :, :dk], before[i])
            joined[i, :, :dk] = both[:, :dk]
            joined[i, :, dk:] = both[:, dk:] + z_ref[h]

        @pl.when(jnp.logical_not(odd))
        def _():
            both = dot(before[i, :, :dk], zb_ref[h])
            joined[i, :, :dk] = both[:, :dk]
            joined[i, :, dk:] = both[:, dk:] + before[i, :, dk:].astype(F32)

        @pl.when(s < 2)
        def _():
            chain[i] = jnp.zeros((dk, dv), BF16)

        @pl.when(s >= 2)
        def _():
            to_chain(i).wait_recv()

        goes[i] = (
            dot(joined[i, :, :dk].astype(BF16), chain[i]) + joined[i, :, dk:]
        ).astype(BF16)

        @pl.when(s < shards - 2)
        def _():
            to_chain(i).start()

    for i in range(share):
        h = mine(i)

        @pl.when(odd)
        def _():
            hands[i] = goes[i]
            joined[i, :, dk:] = (
                dot(before[i, :, :dk], chain[i]) + before[i, :, dk:].astype(F32)
            )

        @pl.when(jnp.logical_not(odd))
        def _():
            hands[i] = (dot(zb_ref[h, :, :dk], chain[i]) + z_ref[h]).astype(BF16)
            joined[i, :, dk:] = chain[i].astype(F32)

        @pl.when(s < shards - 1)
        def _():
            to_next(i).start()

    for i in range(share):
        replay(mine(i), joined[i, :, dk:].astype(BF16))

    for i in range(share):
        @pl.when(s == 0)
        def _():
            came[i] = jnp.zeros((dk, dv), BF16)

        @pl.when(s > 0)
        def _():
            to_next(i).wait_recv()

        replay(theirs(i), came[i])

    def first(j):
        return pltpu.make_async_remote_copy(
            src_ref=give1.at[j], dst_ref=take1.at[j],
            send_sem=send1.at[j], recv_sem=recv1.at[j],
            device_id={"head": mate}, device_id_type=MESH,
        )

    def second(j, step):
        other = (y + step) % pairs
        return pltpu.make_async_remote_copy(
            src_ref=give2.at[j, step - 1], dst_ref=take2.at[j, step - 1],
            send_sem=send2.at[j, step - 1], recv_sem=recv2.at[j, step - 1],
            device_id={"head": other * 2 + c}, device_id_type=MESH,
        )

    def pass_on(j):
        first(j).wait_recv()
        for step in range(1, pairs):
            at = pl.ds(pl.multiple_of(((y + step) % pairs) * rows, rows), rows)
            give2[j, step - 1] = (kept[j, at] + take1[j, at].astype(F32)).astype(BF16)
            second(j, step).start()
        at = pl.ds(pl.multiple_of(y * rows, rows), rows)
        own[j] = kept[j, at] + take1[j, at].astype(F32)

    def project(j, carry):
        pltpu.make_async_copy(
            w_ref.at[:, pl.ds(j * CHUNK, CHUNK)], w_vmem.at[j], w_sem.at[j]
        ).wait()
        give1[j] = dot(normed[:half], w_vmem[j]).astype(BF16)
        first(j).start()
        kept[j] = dot(normed[half:], w_vmem[j])

        @pl.when(j > 0)
        def _():
            pass_on(j - 1)

        return carry

    lax.fori_loop(0, chunks, project, 0)
    pass_on(chunks - 1)

    for j in range(chunks):
        total = own[j]
        for step in range(1, pairs):
            second(j, step).wait_recv()
            total = total + take2[j, step - 1].astype(F32)
        out_ref[:, j * CHUNK:(j + 1) * CHUNK] = total.astype(BF16)

    for j in range(chunks):
        first(j).wait_send()
        for step in range(1, pairs):
            second(j, step).wait_send()

    for i in range(share):
        to_partner(i).wait_send()

    @pl.when(s < shards - 2)
    def _():
        for i in range(share):
            to_chain(i).wait_send()

    @pl.when(s < shards - 1)
    def _():
        for i in range(share):
            to_next(i).wait_send()


def layer(resets, k, q, v, beta, w, shards, groups, heads, dk, dv):
    tokens = beta.shape[1]
    width = w.shape[1]
    chunks = width // CHUNK
    rows = tokens // groups
    pairs = groups // 2
    half = pairs * rows
    far = max(pairs - 1, 1)
    share = heads // 2
    vmem = pl.BlockSpec(memory_space=pltpu.VMEM)
    hbm = pl.BlockSpec(memory_space=pltpu.HBM)
    dma = pltpu.SemaphoreType.DMA
    return pl.pallas_call(
        functools.partial(layer_kernel, shards, groups, heads, dk, dv, chunks),
        in_specs=[hbm, vmem, vmem, vmem, hbm, hbm],
        out_specs=vmem,
        out_shape=jax.ShapeDtypeStruct((rows, width), BF16),
        scratch_shapes=[
            pltpu.VMEM(k.shape, F32),
            pltpu.VMEM(q.shape, F32),
            pltpu.VMEM(v.shape, F32),
            pltpu.SMEM(resets.shape, resets.dtype),
            pltpu.VMEM(beta.shape, beta.dtype),
            pltpu.VMEM((heads, tokens, dk), BF16),
            pltpu.VMEM((heads, tokens, dv), BF16),
            pltpu.VMEM((heads, dk, dv), F32),
            pltpu.VMEM((heads, dk, dk + dv), BF16),
            pltpu.VMEM((chunks, w.shape[0], CHUNK), BF16),
            pltpu.VMEM((share, dk, dk + dv), BF16),
            pltpu.VMEM((share, dk, dk + dv), F32),
            pltpu.VMEM((share, dk, dv), BF16),
            pltpu.VMEM((share, dk, dv), BF16),
            pltpu.VMEM((share, dk, dv), BF16),
            pltpu.VMEM((share, dk, dv), BF16),
            pltpu.VMEM((tokens, heads * dv), BF16),
            pltpu.VMEM((chunks, half, CHUNK), BF16),
            pltpu.VMEM((chunks, half, CHUNK), BF16),
            pltpu.VMEM((chunks, half, CHUNK), F32),
            pltpu.VMEM((chunks, far, rows, CHUNK), BF16),
            pltpu.VMEM((chunks, far, rows, CHUNK), BF16),
            pltpu.VMEM((chunks, rows, CHUNK), F32),
            dma((2,)),
            dma((chunks,)),
            dma((share,)),
            dma((share,)),
            dma((share,)),
            dma((share,)),
            dma((share,)),
            dma((share,)),
            dma((chunks,)),
            dma((chunks,)),
            dma((chunks, far)),
            dma((chunks, far)),
        ],
        compiler_params=pltpu.CompilerParams(
            collective_id=0, has_side_effects=True, vmem_limit_bytes=56 * 1024 * 1024
        ),
        name="layer",
    )(resets, k, q, v, beta, w)


def body(shards, groups, queries, keys, values, beta, reset_blocks, out_weight):
    tokens, heads, dk = queries.shape
    dv = values.shape[2]
    return layer(
        reset_blocks,
        keys.reshape(tokens * heads, dk),
        queries.reshape(tokens * heads, dk),
        values.reshape(tokens, heads, dv // LANES, LANES)
        .transpose(0, 2, 1, 3)
        .reshape(tokens * (dv // LANES) * heads, LANES),
        beta,
        out_weight,
        shards, groups, heads, dk, dv,
    )


def solution(mesh):
    return jax.shard_map(
        functools.partial(body, mesh.shape["seq"], mesh.shape["head"]),
        mesh=mesh,
        in_specs=(
            P("seq", "head", None),
            P("seq", "head", None),
            P("seq", "head", None),
            P("head", "seq"),
            P("seq", None),
            P("head", None),
        ),
        out_specs=P(("seq", "head"), None),
        check_vma=False,
    )
```
